32 devices in a mesh: grp: 2 (over y), seq: 16 (over z, x, core).
Axes of the slice: x: 2, y: 2, z: 4, core: 2. Of those that a mesh axis runs over, the one named last changes fastest.
Arguments:
- queries: bfloat16 [4096, 128], P(('grp', 'seq')), parts along dimension 0, may hold values from -6 to 6
- keys: bfloat16 [4096, 128], P(('grp', 'seq')), parts along dimension 0, may hold values from -6 to 6
- values: bfloat16 [4096, 128], P(('grp', 'seq')), parts along dimension 0, may hold values from -6 to 6
- log_gate: float32 [4096], P(('grp', 'seq')), parts along dimension 0, may hold values from -1 to 0, as said below
- out_grad: bfloat16 [4096, 128], P(('grp', 'seq')), parts along dimension 0, may hold values from -6 to 6
- segment_order: int32 [64], P(('grp', 'seq')), parts along dimension 0, may hold values from 0 to 31, each once
Outputs:
- attn_out: bfloat16 [4096, 128], P(('grp', 'seq')), parts along dimension 0
- query_grad: float32 [4096, 128], P(('grp', 'seq')), parts along dimension 0
- key_grad: float32 [4096, 128], P(('grp', 'seq')), parts along dimension 0
- value_grad: float32 [4096, 128], P(('grp', 'seq')), parts along dimension 0
- gate_grad: float32 [4096], P(('grp', 'seq')), parts along dimension 0
The draws below stay inside these ranges and needn't reach their ends.
There are 2 independent parts, one for each index of `grp`. The reference program is written for one: setup_inputs(seed, part) draws one part's arguments, and reference() takes and returns one part's arrays. A program takes and returns all parts, laid end to end along the dimension named above; each array names one. Nothing has to cross between parts.
Inputs may be any that keep to these rules, and one draw needn't show every extreme that they name: `log_gate`: every gate is below one. `segment_order`: each segment index appears once.
All inputs are finite; a program needn't handle non-finite values.
Results may differ from the reference program's by a relative error of at most 0.0095.
Values may be sent and summed in bfloat16 or wider, within the bound.
A program may use at most 64 MiB of HBM per device.

```python
import jax
import jax.numpy as jnp
from jax import lax

DH = 128
PIECE_LENGTH = 64
SEGMENTS = 32
STREAM_LENGTH = 2048


def paired_rows(key):
    key_one, key_two = jax.random.split(jax.random.fold_in(key, 7), 2)
    query_rows = jnp.clip(1.6 * jax.random.normal(key_one, (STREAM_LENGTH, DH), jnp.float32), -6.0, 6.0)
    key_rows = jnp.clip(1.6 * jax.random.normal(key_two, (STREAM_LENGTH, DH), jnp.float32), -6.0, 6.0)
    return (query_rows, key_rows)


def draw_queries(key, part):
    return paired_rows(key)[0].astype(jnp.bfloat16)


def draw_keys(key, part):
    return paired_rows(key)[1].astype(jnp.bfloat16)


def draw_log_gate(key, part):
    base_key, factor_key, jump_place_seed, jump_size_seed = jax.random.split(jax.random.fold_in(key, 11), 4)
    lowest = 0.1 / STREAM_LENGTH
    highest = 2.0 / STREAM_LENGTH
    baseline_decay_level = jnp.exp(jax.random.uniform(base_key, (STREAM_LENGTH,), jnp.float32, jnp.log(lowest), jnp.log(highest)))
    forget_multiplier = jnp.exp(jax.random.uniform(factor_key, (STREAM_LENGTH // PIECE_LENGTH, 1), jnp.float32, jnp.log(0.4), jnp.log(2.5)))
    jump_positions_list = jax.random.randint(jump_place_seed, (3,), 0, STREAM_LENGTH)
    jump_sizes = jax.random.uniform(jump_size_seed, (3,), jnp.float32, 0.2, 0.5)
    jump_count = jnp.zeros((STREAM_LENGTH,), jnp.float32).at[jump_positions_list].add(jump_sizes)
    return -((baseline_decay_level.reshape(-1, PIECE_LENGTH) * forget_multiplier).reshape(-1) + jump_count)


def levels(stream_key, extent, cuts, low, top_value):
    level = 1.0
    for position, parts in cuts:
        steps = jax.random.uniform(jax.random.fold_in(jax.random.fold_in(stream_key, 6), position), (parts,), jnp.float32, low / len(cuts), top_value / len(cuts))
        level = level * jnp.repeat(jnp.exp(steps), extent[position] // parts).reshape((-1,) + (1,) * (len(extent) - 1 - position))
    return level


def scatter_about(key, extent, spread, bound, pieces=(), kind=jnp.bfloat16):
    result = jax.random.normal(key, extent, jnp.float32) * spread
    if len(pieces) > 0:
        result = levels(key, extent, pieces, -0.22, 0.18) * result
    return jnp.clip(result, min=-bound, max=bound).astype(kind)


def setup_inputs(seed: int = 0, part: int = 0) -> dict:
    key_of = jax.random.split(jax.random.key(seed), 7)
    part_splits = jax.random.split(jax.random.fold_in(key_of[6], part), 7)
    return {
        "queries": draw_queries(jax.random.fold_in(jax.random.fold_in(key_of[6], part), 71), part),
        "keys": draw_keys(jax.random.fold_in(jax.random.fold_in(key_of[6], part), 71), part),
        "values": scatter_about(part_splits[2], (STREAM_LENGTH, DH), 1.0, 6.0, ((0, 16),)),
        "log_gate": draw_log_gate(jax.random.fold_in(jax.random.fold_in(key_of[6], part), 71), part),
        "out_grad": scatter_about(part_splits[4], (STREAM_LENGTH, DH), 1.0, 6.0, ((0, 16),)),
        "segment_order": jax.random.permutation(part_splits[5], SEGMENTS).astype(jnp.int32),
    }


masked_value = -1e30


def reference(queries, keys, values, log_gate, out_grad, segment_order):
    total_len, width = queries.shape
    segment_rows = total_len // segment_order.shape[0]
    score_scale = width ** -0.5
    true_order = jnp.argsort(segment_order).astype(jnp.int32)
    offsets_in = jnp.arange(segment_rows, dtype=jnp.int32)
    positions = (segment_order[:, None] * segment_rows + offsets_in[None, :]).reshape(-1)
    ordered = log_gate.reshape(-1, segment_rows)[true_order].reshape(-1)
    gate_cum = jnp.cumsum(ordered).reshape(-1, segment_rows)[segment_order].reshape(-1)
    block = 1024 if total_len % 1024 == 0 else total_len
    count = total_len // block

    def block_scores(block_index):
        start = (block_index * block).astype(jnp.int32)
        rows = lax.dynamic_slice_in_dim(queries, start, block)
        row_gate = lax.dynamic_slice_in_dim(gate_cum, start, block)
        row_pos = lax.dynamic_slice_in_dim(positions, start, block)
        scores = jnp.dot(rows, keys.T, preferred_element_type=jnp.float32) * score_scale
        scores = scores + row_gate[:, None] - gate_cum[None, :]
        visible = positions[None, :] <= row_pos[:, None]
        return rows, jnp.where(visible, scores, masked_value)

    def forward_block(block_index):
        rows, kept = block_scores(block_index)
        top = jnp.max(kept, axis=1)
        log_total = top + jnp.log(jnp.sum(jnp.exp(kept - top[:, None]), axis=1))
        probs = jnp.exp(kept - log_total[:, None]).astype(jnp.bfloat16)
        return jnp.dot(probs, values, preferred_element_type=jnp.float32), log_total

    indices = jnp.arange(count, dtype=jnp.int32)
    out_blocks, total_blocks = lax.map(forward_block, indices)
    out_full = out_blocks.reshape(total_len, width)
    log_total = total_blocks.reshape(-1)
    attn_out = out_full.astype(jnp.bfloat16)
    row_delta = jnp.sum(out_grad.astype(jnp.float32) * out_full, axis=1)

    def backward_block(carry, block_index):
        key_acc, value_acc, column_acc = carry
        start = (block_index * block).astype(jnp.int32)
        rows, kept = block_scores(block_index)
        grad_rows = lax.dynamic_slice_in_dim(out_grad, start, block)
        row_total = lax.dynamic_slice_in_dim(log_total, start, block)
        delta_rows = lax.dynamic_slice_in_dim(row_delta, start, block)
        probs = jnp.exp(kept - row_total[:, None])
        dprob = jnp.dot(grad_rows, values.T, preferred_element_type=jnp.float32)
        dscore = probs * (dprob - delta_rows[:, None])
        low = dscore.astype(jnp.bfloat16)
        query_rows_grad = jnp.dot(low, keys, preferred_element_type=jnp.float32) * score_scale
        key_acc = key_acc + jnp.dot(low.T, rows, preferred_element_type=jnp.float32) * score_scale
        value_acc = value_acc + jnp.dot(probs.astype(jnp.bfloat16).T, grad_rows, preferred_element_type=jnp.float32)
        column_acc = column_acc + jnp.sum(dscore, axis=0)
        return (key_acc, value_acc, column_acc), query_rows_grad

    zeros_rows = jnp.zeros((total_len, width), jnp.float32)
    carry_init = (zeros_rows, zeros_rows, jnp.zeros((total_len,), jnp.float32))
    (key_grad, value_grad, column_acc), query_blocks = lax.scan(backward_block, carry_init, indices)
    query_grad = query_blocks.reshape(total_len, width)
    gate_point = -column_acc
    ordered_point = gate_point.reshape(-1, segment_rows)[true_order].reshape(-1)
    suffix = jnp.flip(jnp.cumsum(jnp.flip(ordered_point)))
    gate_grad = suffix.reshape(-1, segment_rows)[segment_order].reshape(-1)
    return attn_out, query_grad, key_grad, value_grad, gate_grad
```

```python
import functools
import math

import jax
import jax.numpy as jnp
from jax import lax
from jax.experimental import pallas as pl
from jax.experimental.pallas import tpu as pltpu
from jax.sharding import PartitionSpec as P

MESH = pl.DeviceIdType.MESH
HIDDEN = -1e30
FLOOR = -1e29
LOG2E = math.log2(math.e)


def dot(left, right, left_dim, right_dim):
    return lax.dot_general(
        left, right, (((left_dim,), (right_dim,)), ((), ())), preferred_element_type=jnp.float32
    )


def for_each(count, body):
    if count <= 4:
        for index in range(count):
            body(index)
    else:
        lax.fori_loop(0, count, lambda index, carry: (body(index), carry)[1], 0)


def kernel(
    rows,
    cols,
    halves,
    q_hbm,
    k_hbm,
    v_hbm,
    gate_hbm,
    g_hbm,
    order_ref,
    out_ref,
    dq_ref,
    dk_ref,
    dv_ref,
    dgate_ref,
    gate_ref,
    load_sems,
    meta,
    pts_out,
    pts_in,
    cum,
    place,
    q_all,
    g_all,
    k_all,
    v_all,
    p_all,
    dp_all,
    part_stat,
    stats,
    deltas,
    p_low,
    ds_low,
    dk_out,
    dv_out,
    dk_in,
    dv_in,
    o_out,
    dq_out,
    o_in,
    dq_in,
    meta_send,
    meta_recv,
    pts_send,
    pts_recv,
    q_send,
    q_recv,
    k_send,
    k_recv,
    stat_send,
    stat_recv,
    delta_send,
    delta_recv,
    kout_send,
    kout_recv,
    qout_send,
    qout_recv,
):
    devices = rows * cols
    tokens, width = q_hbm.shape
    piece = tokens // halves
    queries = cols * tokens
    scale = width ** (-0.5)
    grp = lax.axis_index("grp")
    me = lax.axis_index("seq")
    my_row = me // cols
    my_col = me % cols

    def at(index):
        return (grp, index)

    def other(shift):
        return lax.rem(me + shift, devices)

    def in_row(shift):
        return my_row * cols + lax.rem(my_col + shift, cols)

    def in_column(shift):
        return lax.rem(my_row + shift, rows) * cols + my_col

    barrier = pltpu.get_barrier_semaphore()

    def greet(shift):
        pl.semaphore_signal(barrier, inc=1, device_id=at(other(shift + 1)), device_id_type=MESH)

    lax.fori_loop(0, devices - 1, lambda i, c: (greet(i), c)[1], 0)

    q_ref, g_ref, k_ref, v_ref = q_all.at[0], g_all.at[0], k_all.at[0], v_all.at[0]
    loads = [
        pltpu.make_async_copy(source, target, load_sems.at[index])
        for index, (source, target) in enumerate(
            (
                (gate_hbm, gate_ref),
                (q_hbm, q_ref),
                (k_hbm, k_ref),
                (g_hbm, g_ref),
                (v_hbm, v_ref),
            )
        )
    ]
    for load in loads:
        load.start()
    loads[0].wait()

    lane = lax.broadcasted_iota(jnp.int32, (tokens, tokens), 1)
    line = lax.broadcasted_iota(jnp.int32, (tokens, tokens), 0)
    same = lane // piece == line // piece
    diagonal = lane == line

    def to_column(row):
        return jnp.sum(jnp.where(diagonal, row, 0.0), axis=1, keepdims=True)

    def to_row(column):
        return jnp.sum(jnp.where(diagonal, column, 0.0), axis=0, keepdims=True)

    gate_row = gate_ref[...].reshape(1, tokens)
    local_cum = jnp.sum(
        jnp.where(same & (line <= lane), to_column(gate_row), 0.0), axis=0, keepdims=True
    )
    lane_row = lax.broadcasted_iota(jnp.int32, (1, tokens), 1)
    own_order = jnp.zeros((1, tokens), jnp.float32)
    for half in range(halves):
        own_order = jnp.where(
            lane_row // piece == half, order_ref[half].astype(jnp.float32), own_order
        )
    meta[pl.ds(me, 1), 0:1, :] = local_cum.reshape(1, 1, tokens)
    meta[pl.ds(me, 1), 1:2, :] = own_order.reshape(1, 1, tokens)
    for load in loads[1:]:
        load.wait()

    pl.semaphore_wait(barrier, devices - 1)

    def meta_copy(shift):
        return pltpu.make_async_remote_copy(
            src_ref=meta.at[me],
            dst_ref=meta.at[me],
            send_sem=meta_send.at[shift],
            recv_sem=meta_recv.at[shift],
            device_id=at(other(shift)),
            device_id_type=MESH,
        )

    def meta_arrival(shift):
        source = lax.rem(me + devices - shift, devices)
        return pltpu.make_async_remote_copy(
            src_ref=meta.at[source],
            dst_ref=meta.at[source],
            send_sem=meta_send.at[shift],
            recv_sem=meta_recv.at[shift],
            device_id=at(other(shift)),
            device_id_type=MESH,
        )

    def row_copy(which, shift):
        ref, slots = ((q_ref, q_all), (g_ref, g_all))[which]
        return pltpu.make_async_remote_copy(
            src_ref=ref,
            dst_ref=slots.at[cols - shift],
            send_sem=q_send.at[which, shift],
            recv_sem=q_recv.at[which, cols - shift],
            device_id=at(in_row(shift)),
            device_id_type=MESH,
        )

    def column_copy(which, shift):
        ref, slots = ((k_ref, k_all), (v_ref, v_all))[which]
        return pltpu.make_async_remote_copy(
            src_ref=ref,
            dst_ref=slots.at[rows - shift],
            send_sem=k_send.at[which, shift],
            recv_sem=k_recv.at[which, rows - shift],
            device_id=at(in_column(shift)),
            device_id_type=MESH,
        )

    lax.fori_loop(1, devices, lambda i, c: (meta_copy(i).start(), c)[1], 0)
    for which in range(2):
        for shift in range(1, cols):
            row_copy(which, shift).start()
        for shift in range(1, rows):
            column_copy(which, shift).start()

    lax.fori_loop(1, devices, lambda i, c: (meta_arrival(i).wait_recv(), c)[1], 0)

    orders = meta[:, 1, :]
    base = meta[:, 0, :]
    total = base
    for half in range(halves):
        totals = base[:, (half + 1) * piece - 1 : (half + 1) * piece]
        heads = orders[:, half * piece : half * piece + 1]

        for device in range(devices):
            earlier = heads[device : device + 1, :] < orders
            total = total + jnp.where(earlier, totals[device : device + 1, :], 0.0)
    cum[...] = total * LOG2E
    within = (lax.broadcasted_iota(jnp.int32, (devices, tokens), 1) % piece).astype(jnp.float32)
    place[...] = orders * piece + within

    query_cum = jnp.concatenate([cum[pl.ds(in_row(s), 1), :] for s in range(cols)], axis=1)
    query_place = jnp.concatenate([place[pl.ds(in_row(s), 1), :] for s in range(cols)], axis=1)

    for shift in range(1, cols):
        row_copy(0, cols - shift).wait_recv()

    def first_pass(slot):
        source = in_column(slot)
        key_cum = to_column(cum[pl.ds(source, 1), :])
        key_place = to_column(place[pl.ds(source, 1), :])
        if isinstance(slot, int) and slot == 0:
            pass
        else:
            arrived(0, slot)
        scores = dot(k_all[slot], q_all[...].reshape(queries, width), 1, 1)
        scores = scores * (scale * LOG2E) + (query_cum - key_cum)
        scores = jnp.where(key_place <= query_place, scores, HIDDEN)
        top = jnp.maximum(jnp.max(scores, axis=0, keepdims=True), FLOOR)
        probs = jnp.exp2(scores - top)
        p_all[slot] = probs
        part_stat[slot, 0:1, :] = top
        part_stat[slot, 1:2, :] = jnp.sum(probs, axis=0, keepdims=True)

    def arrived(which, slot):
        ref, slots = ((k_ref, k_all), (v_ref, v_all))[which]
        pltpu.make_async_remote_copy(
            src_ref=ref,
            dst_ref=slots.at[slot],
            send_sem=k_send.at[which, slot],
            recv_sem=k_recv.at[which, slot],
            device_id=at(in_column(slot)),
            device_id_type=MESH,
        ).wait_recv()

    first_pass(0)
    for_each(rows - 1, lambda i: first_pass(i + 1))

    tops = part_stat[:, 0, :]
    top = jnp.max(tops, axis=0, keepdims=True)
    shrink = jnp.exp2(tops - top)
    stats[0, 0:1, :] = top
    stats[0, 1:2, :] = jnp.sum(part_stat[:, 1, :] * shrink, axis=0, keepdims=True)

    def stat_copy(shift):
        return pltpu.make_async_remote_copy(
            src_ref=stats.at[0],
            dst_ref=stats.at[cols - shift],
            send_sem=stat_send.at[shift],
            recv_sem=stat_recv.at[cols - shift],
            device_id=at(in_row(shift)),
            device_id_type=MESH,
        )

    for shift in range(1, cols):
        stat_copy(shift).start()

    for shift in range(1, cols):
        row_copy(1, cols - shift).wait_recv()
    for shift in range(1, cols):
        stat_copy(cols - shift).wait_recv()

    def turn(turned, slot):
        cut = (cols - slot) * tokens
        return jnp.concatenate([turned[:, cut:], turned[:, :cut]], axis=1)

    aligned = [stats[0]] + [turn(stats[slot], slot) for slot in range(1, cols)]
    top = functools.reduce(jnp.maximum, [part[0:1, :] for part in aligned])
    sums = functools.reduce(
        jnp.add, [jnp.exp2(part[0:1, :] - top) * part[1:2, :] for part in aligned]
    )
    inverse = 1.0 / sums

    def normalise(slot):
        if not (isinstance(slot, int) and slot == 0):
            arrived(1, slot)
        dprobs = dot(v_all[slot], g_all[...].reshape(queries, width), 1, 1)
        probs = p_all[slot] * (jnp.exp2(part_stat[slot, 0:1, :] - top) * inverse)
        low = probs.astype(jnp.bfloat16)
        p_all[slot] = probs
        p_low[slot] = low
        dp_all[slot] = dprobs
        part_stat[slot, 2:3, :] = jnp.sum(
            low.astype(jnp.float32) * dprobs, axis=0, keepdims=True
        )

    normalise(0)
    for_each(rows - 1, lambda i: normalise(i + 1))
    deltas[0] = jnp.sum(part_stat[:, 2, :], axis=0, keepdims=True)

    def delta_copy(shift):
        return pltpu.make_async_remote_copy(
            src_ref=deltas.at[0],
            dst_ref=deltas.at[cols - shift],
            send_sem=delta_send.at[shift],
            recv_sem=delta_recv.at[cols - shift],
            device_id=at(in_row(shift)),
            device_id_type=MESH,
        )

    for shift in range(1, cols):
        delta_copy(shift).start()

    def column_out(which, slot):
        source, target = ((dk_out, dk_in), (dv_out, dv_in))[which]
        return pltpu.make_async_remote_copy(
            src_ref=source.at[slot],
            dst_ref=target.at[rows - slot],
            send_sem=kout_send.at[which, slot],
            recv_sem=kout_recv.at[which, rows - slot],
            device_id=at(in_column(slot)),
            device_id_type=MESH,
        )

    def value_pass(slot):
        value_part = dot(p_low[slot], g_all[...].reshape(queries, width), 1, 0)
        if isinstance(slot, int) and slot == 0:
            dv_ref[...] = value_part
        else:
            dv_out[slot] = value_part.astype(jnp.bfloat16)
            column_out(1, slot).start()

    for_each(rows - 1, lambda i: value_pass(i + 1))

    def row_out(which, slot):
        source, target = ((o_out, o_in), (dq_out, dq_in))[which]
        return pltpu.make_async_remote_copy(
            src_ref=source.at[slot],
            dst_ref=target.at[cols - slot],
            send_sem=qout_send.at[which, slot],
            recv_sem=qout_recv.at[which, cols - slot],
            device_id=at(in_row(slot)),
            device_id_type=MESH,
        )

    p_flat = p_low[...].reshape(rows * tokens, queries)
    v_flat = v_all[...].reshape(rows * tokens, width)
    out_part = dot(v_flat, p_flat, 0, 0)
    for slot in range(1, cols):
        o_out[slot] = out_part[:, slot * tokens : (slot + 1) * tokens].astype(jnp.bfloat16)
        row_out(0, slot).start()

    for shift in range(1, cols):
        delta_copy(cols - shift).wait_recv()
    delta = deltas[0]
    for slot in range(1, cols):
        delta = delta + turn(deltas[slot], slot)

    def second_pass(slot):
        dscore = p_all[slot] * (dp_all[slot] - delta)
        ds = dscore.astype(jnp.bfloat16)
        ds_low[slot] = ds
        key_part = dot(ds, q_all[...].reshape(queries, width), 1, 0) * scale
        points = -to_row(jnp.sum(dscore, axis=1, keepdims=True))
        if isinstance(slot, int):
            pts_out[slot : slot + 1, :] = points
        else:
            pts_out[pl.ds(slot, 1), :] = points
        if isinstance(slot, int) and slot == 0:
            dk_ref[...] = key_part
        else:
            dk_out[slot] = key_part.astype(jnp.bfloat16)
            column_out(0, slot).start()

    for_each(rows - 1, lambda i: second_pass(i + 1))
    second_pass(0)
    value_pass(0)

    def pts_copy(shift):
        return pltpu.make_async_remote_copy(
            src_ref=pts_out,
            dst_ref=pts_in.at[me],
            send_sem=pts_send.at[shift],
            recv_sem=pts_recv.at[shift],
            device_id=at(other(shift)),
            device_id_type=MESH,
        )

    def pts_arrival(shift):
        source = lax.rem(me + devices - shift, devices)
        return pltpu.make_async_remote_copy(
            src_ref=pts_out,
            dst_ref=pts_in.at[source],
            send_sem=pts_send.at[shift],
            recv_sem=pts_recv.at[shift],
            device_id=at(other(shift)),
            device_id_type=MESH,
        )

    lax.fori_loop(1, devices, lambda i, c: (pts_copy(i).start(), c)[1], 0)
    pts_in[pl.ds(me, 1)] = pts_out[...].reshape(1, *pts_out.shape)

    ds_flat = ds_low[...].reshape(rows * tokens, queries)
    k_flat = k_all[...].reshape(rows * tokens, width)
    query_part = dot(k_flat, ds_flat, 0, 0) * scale
    for slot in range(1, cols):
        dq_out[slot] = query_part[:, slot * tokens : (slot + 1) * tokens].astype(jnp.bfloat16)
        row_out(1, slot).start()

    for slot in range(1, cols):
        row_out(0, cols - slot).wait_recv()
    out_sum = out_part[:, :tokens]
    for slot in range(1, cols):
        out_sum = out_sum + o_in[slot].astype(jnp.float32)
    out_ref[...] = jnp.transpose(out_sum).astype(out_ref.dtype)

    lax.fori_loop(1, devices, lambda i, c: (pts_arrival(i).wait_recv(), c)[1], 0)

    def add_points(index, carry):
        later, own = carry
        row = index // cols
        col = index % cols
        point = jnp.zeros((1, tokens), jnp.float32)
        for s in range(rows):
            giver = lax.rem(row + rows - s, rows) * cols + col
            point = point + pts_in[giver, s : s + 1, :]
        their_order = meta[index, 1:2, :]
        for half in range(halves):
            later[half] = later[half] + jnp.where(
                their_order > order_ref[half].astype(jnp.float32), point, 0.0
            )
        return (later, jnp.where(index == me, point, own))

    carry = ([jnp.zeros((1, tokens), jnp.float32) for _ in range(halves)],) + (
        jnp.zeros((1, tokens), jnp.float32),
    )
    if devices <= 16:
        for index in range(devices):
            carry = add_points(index, carry)
    else:
        carry = lax.fori_loop(0, devices, add_points, carry)
    later, own = carry
    gate_grad = jnp.sum(jnp.where(same & (line >= lane), to_column(own), 0.0), axis=0, keepdims=True)
    for half in range(halves):
        rest = jnp.sum(later[half], axis=1, keepdims=True)
        gate_grad = jnp.where(lane_row // piece == half, gate_grad + rest, gate_grad)
    dgate_ref[...] = gate_grad.reshape(tokens)

    for slot in range(1, cols):
        row_out(1, cols - slot).wait_recv()
    query_sum = query_part[:, :tokens]
    for slot in range(1, cols):
        query_sum = query_sum + dq_in[slot].astype(jnp.float32)
    dq_ref[...] = jnp.transpose(query_sum)

    for which, target in enumerate((dk_ref, dv_ref)):
        for slot in range(1, rows):
            column_out(which, rows - slot).wait_recv()
        for slot in range(1, rows):
            target[...] += (dk_in, dv_in)[which][slot].astype(jnp.float32)

    lax.fori_loop(1, devices, lambda i, c: (meta_copy(i).wait_send(), c)[1], 0)
    lax.fori_loop(1, devices, lambda i, c: (pts_copy(i).wait_send(), c)[1], 0)
    for which in range(2):
        for shift in range(1, cols):
            row_copy(which, shift).wait_send()
            row_out(which, shift).wait_send()
        for shift in range(1, rows):
            column_copy(which, shift).wait_send()
            column_out(which, shift).wait_send()
    for shift in range(1, cols):
        stat_copy(shift).wait_send()
        delta_copy(shift).wait_send()


def hand_on(count, *refs):
    sources, targets, sems = refs[:count], refs[count : 2 * count], refs[2 * count]
    copies = [
        pltpu.make_async_copy(source, target, sems.at[index])
        for index, (source, target) in enumerate(zip(sources, targets))
    ]
    for copy in copies:
        copy.start()
    for copy in copies:
        copy.wait()


def local(rows, cols, queries, keys, values, log_gate, out_grad, segment_order):
    tokens, width = queries.shape
    halves = segment_order.shape[0]
    devices = rows * cols
    across = cols * tokens
    low, full = jnp.bfloat16, jnp.float32
    dma = pltpu.SemaphoreType.DMA
    in_vmem = pl.BlockSpec(memory_space=pltpu.VMEM)
    in_hbm = pl.BlockSpec(memory_space=pltpu.HBM)
    shapes = (
        jax.ShapeDtypeStruct((tokens, width), low),
        jax.ShapeDtypeStruct((tokens, width), full),
        jax.ShapeDtypeStruct((tokens, width), full),
        jax.ShapeDtypeStruct((tokens, width), full),
        jax.ShapeDtypeStruct((tokens,), full),
    )
    results = pl.pallas_call(
        functools.partial(kernel, rows, cols, halves),
        out_shape=tuple(pltpu.VMEM(shape.shape, shape.dtype) for shape in shapes),
        in_specs=[in_hbm] * 5 + [pl.BlockSpec(memory_space=pltpu.SMEM)],
        out_specs=[in_vmem] * 5,
        scratch_shapes=[
            pltpu.VMEM((tokens,), full),
            dma((5,)),
            pltpu.VMEM((devices, 2, tokens), full),
            pltpu.VMEM((rows, tokens), full),
            pltpu.VMEM((devices, rows, tokens), full),
            pltpu.VMEM((devices, tokens), full),
            pltpu.VMEM((devices, tokens), full),
            pltpu.VMEM((cols, tokens, width), low),
            pltpu.VMEM((cols, tokens, width), low),
            pltpu.VMEM((rows, tokens, width), low),
            pltpu.VMEM((rows, tokens, width), low),
            pltpu.VMEM((rows, tokens, across), full),
            pltpu.VMEM((rows, tokens, across), full),
            pltpu.VMEM((rows, 8, across), full),
            pltpu.VMEM((cols, 4, across), full),
            pltpu.VMEM((cols, 1, across), full),
            pltpu.VMEM((rows, tokens, across), low),
            pltpu.VMEM((rows, tokens, across), low),
            pltpu.VMEM((rows, tokens, width), low),
            pltpu.VMEM((rows, tokens, width), low),
            pltpu.VMEM((rows, tokens, width), low),
            pltpu.VMEM((rows, tokens, width), low),
            pltpu.VMEM((cols, tokens, width), low),
            pltpu.VMEM((cols, tokens, width), low),
            pltpu.VMEM((cols, tokens, width), low),
            pltpu.VMEM((cols, tokens, width), low),
            dma((devices,)),
            dma((devices,)),
            dma((devices,)),
            dma((devices,)),
            dma((2, cols)),
            dma((2, cols)),
            dma((2, rows)),
            dma((2, rows)),
            dma((cols,)),
            dma((cols,)),
            dma((cols,)),
            dma((cols,)),
            dma((2, rows)),
            dma((2, rows)),
            dma((2, cols)),
            dma((2, cols)),
        ],
        compiler_params=pltpu.CompilerParams(
            collective_id=0, has_side_effects=True, vmem_limit_bytes=60 * 1024 * 1024
        ),
    )(queries, keys, values, log_gate, out_grad, segment_order)
    return pl.pallas_call(
        functools.partial(hand_on, len(shapes)),
        out_shape=shapes,
        in_specs=[in_vmem] * len(shapes),
        out_specs=[in_hbm] * len(shapes),
        scratch_shapes=[dma((len(shapes),))],
    )(*results)


def solution(mesh):
    devices = mesh.shape["seq"]
    cols = max(c for c in range(1, math.isqrt(devices) + 1) if devices % c == 0)
    flat = P(("grp", "seq"))
    wide = P(("grp", "seq"), None)
    return jax.shard_map(
        functools.partial(local, devices // cols, cols),
        mesh=mesh,
        in_specs=(wide, wide, wide, flat, wide, flat),
        out_specs=(wide, wide, wide, wide, flat),
        check_vma=False,
    )
```

```python
import functools
import math

import jax
import jax.numpy as jnp
from jax import lax
from jax.experimental import pallas as pl
from jax.experimental.pallas import tpu as pltpu
from jax.sharding import PartitionSpec as P

MESH = pl.DeviceIdType.MESH
HIDDEN = -1e30
FLOOR = -1e29
LOG2E = math.log2(math.e)


def dot(left, right, left_dim, right_dim):
    return lax.dot_general(
        left, right, (((left_dim,), (right_dim,)), ((), ())), preferred_element_type=jnp.float32
    )


def for_each(count, body):
    if count <= 4:
        for index in range(count):
            body(index)
    else:
        lax.fori_loop(0, count, lambda index, carry: (body(index), carry)[1], 0)


def kernel(
    rows,
    cols,
    halves,
    q_hbm,
    k_hbm,
    v_hbm,
    gate_hbm,
    g_hbm,
    order_ref,
    out_ref,
    dq_ref,
    dk_ref,
    dv_ref,
    dgate_ref,
    gate_ref,
    load_sems,
    meta,
    pts_in,
    cum,
    place,
    q_all,
    g_all,
    k_all,
    v_all,
    p_all,
    dp_all,
    part_stat,
    stats,
    deltas,
    p_low,
    ds_low,
    dk_out,
    dv_out,
    dk_in,
    dv_in,
    o_out,
    dq_out,
    o_in,
    dq_in,
    meta_send,
    meta_recv,
    pts_send,
    pts_recv,
    q_send,
    q_recv,
    k_send,
    k_recv,
    stat_send,
    stat_recv,
    delta_send,
    delta_recv,
    kout_send,
    kout_recv,
    qout_send,
    qout_recv,
):
    devices = rows * cols
    tokens, width = q_hbm.shape
    piece = tokens // halves
    queries = cols * tokens
    scale = width ** (-0.5)
    grp = lax.axis_index("grp")
    me = lax.axis_index("seq")
    my_row = me // cols
    my_col = me % cols

    def at(index):
        return (grp, index)

    def other(shift):
        return lax.rem(me + shift, devices)

    def slot_of(index):
        return lax.rem(me + devices - index, devices)

    def arrive(slots, sem):
        rest = slots.at[pl.ds(1, slots.shape[0] - 1)]
        pltpu.make_async_copy(rest, rest, sem).wait()

    def in_row(shift):
        return my_row * cols + lax.rem(my_col + shift, cols)

    def in_column(shift):
        return lax.rem(my_row + shift, rows) * cols + my_col

    barrier = pltpu.get_barrier_semaphore()

    def greet(shift):
        pl.semaphore_signal(barrier, inc=1, device_id=at(other(shift + 1)), device_id_type=MESH)

    lax.fori_loop(0, devices - 1, lambda i, c: (greet(i), c)[1], 0)

    q_ref, g_ref, k_ref, v_ref = q_all.at[0], g_all.at[0], k_all.at[0], v_all.at[0]
    loads = [
        pltpu.make_async_copy(source, target, load_sems.at[index])
        for index, (source, target) in enumerate(
            (
                (gate_hbm, gate_ref),
                (q_hbm, q_ref),
                (k_hbm, k_ref),
                (g_hbm, g_ref),
                (v_hbm, v_ref),
            )
        )
    ]
    for load in loads:
        load.start()
    loads[0].wait()

    lane = lax.broadcasted_iota(jnp.int32, (tokens, tokens), 1)
    line = lax.broadcasted_iota(jnp.int32, (tokens, tokens), 0)
    same = lane // piece == line // piece
    diagonal = lane == line

    def to_column(row):
        return jnp.sum(jnp.where(diagonal, row, 0.0), axis=1, keepdims=True)

    def to_row(column):
        return jnp.sum(jnp.where(diagonal, column, 0.0), axis=0, keepdims=True)

    gate_row = gate_ref[...].reshape(1, tokens)
    local_cum = jnp.sum(
        jnp.where(same & (line <= lane), to_column(gate_row), 0.0), axis=0, keepdims=True
    )
    lane_row = lax.broadcasted_iota(jnp.int32, (1, tokens), 1)
    own_order = jnp.zeros((1, tokens), jnp.float32)
    for half in range(halves):
        own_order = jnp.where(
            lane_row // piece == half, order_ref[half].astype(jnp.float32), own_order
        )
    meta[0, 0:1, :] = local_cum
    meta[0, 1:2, :] = own_order
    for load in loads[1:]:
        load.wait()

    pl.semaphore_wait(barrier, devices - 1)

    def meta_copy(shift):
        return pltpu.make_async_remote_copy(
            src_ref=meta.at[0],
            dst_ref=meta.at[shift],
            send_sem=meta_send,
            recv_sem=meta_recv,
            device_id=at(other(shift)),
            device_id_type=MESH,
        )

    def row_copy(which, shift):
        ref, slots = ((q_ref, q_all), (g_ref, g_all))[which]
        return pltpu.make_async_remote_copy(
            src_ref=ref,
            dst_ref=slots.at[cols - shift],
            send_sem=q_send.at[which],
            recv_sem=q_recv.at[which],
            device_id=at(in_row(shift)),
            device_id_type=MESH,
        )

    def column_copy(which, shift):
        ref, slots = ((k_ref, k_all), (v_ref, v_all))[which]
        return pltpu.make_async_remote_copy(
            src_ref=ref,
            dst_ref=slots.at[rows - shift],
            send_sem=k_send.at[which],
            recv_sem=k_recv.at[which, rows - shift],
            device_id=at(in_column(shift)),
            device_id_type=MESH,
        )

    for shift in range(1, rows):
        column_copy(0, shift).start()
    for shift in range(1, cols):
        row_copy(0, shift).start()
    lax.fori_loop(1, devices, lambda i, c: (meta_copy(i).start(), c)[1], 0)
    for shift in range(1, rows):
        column_copy(1, shift).start()
    for shift in range(1, cols):
        row_copy(1, shift).start()

    arrive(meta, meta_recv)

    orders = meta[:, 1, :]
    base = meta[:, 0, :]
    total = base
    for half in range(halves):
        totals = base[:, (half + 1) * piece - 1 : (half + 1) * piece]
        heads = orders[:, half * piece : half * piece + 1]

        for device in range(devices):
            earlier = heads[device : device + 1, :] < orders
            total = total + jnp.where(earlier, totals[device : device + 1, :], 0.0)
    cum[...] = total * LOG2E
    within = (lax.broadcasted_iota(jnp.int32, (devices, tokens), 1) % piece).astype(jnp.float32)
    place[...] = orders * piece + within

    query_cum = jnp.concatenate([cum[pl.ds(slot_of(in_row(s)), 1), :] for s in range(cols)], axis=1)
    query_place = jnp.concatenate([place[pl.ds(slot_of(in_row(s)), 1), :] for s in range(cols)], axis=1)

    arrive(q_all, q_recv.at[0])

    def first_pass(slot):
        source = slot_of(in_column(slot))
        key_cum = to_column(cum[pl.ds(source, 1), :])
        key_place = to_column(place[pl.ds(source, 1), :])
        if isinstance(slot, int) and slot == 0:
            pass
        else:
            arrived(0, slot)
        scores = dot(k_all[slot], q_all[...].reshape(queries, width), 1, 1)
        scores = scores * (scale * LOG2E) + (query_cum - key_cum)
        scores = jnp.where(key_place <= query_place, scores, HIDDEN)
        top = jnp.maximum(jnp.max(scores, axis=0, keepdims=True), FLOOR)
        probs = jnp.exp2(scores - top)
        p_all[slot] = probs
        part_stat[slot, 0:1, :] = top
        part_stat[slot, 1:2, :] = jnp.sum(probs, axis=0, keepdims=True)

    def arrived(which, slot):
        ref, slots = ((k_ref, k_all), (v_ref, v_all))[which]
        pltpu.make_async_remote_copy(
            src_ref=ref,
            dst_ref=slots.at[slot],
            send_sem=k_send.at[which],
            recv_sem=k_recv.at[which, slot],
            device_id=at(in_column(slot)),
            device_id_type=MESH,
        ).wait_recv()

    first_pass(0)
    for_each(rows - 1, lambda i: first_pass(i + 1))

    tops = part_stat[:, 0, :]
    top = jnp.max(tops, axis=0, keepdims=True)
    shrink = jnp.exp2(tops - top)
    stats[0, 0:1, :] = top
    stats[0, 1:2, :] = jnp.sum(part_stat[:, 1, :] * shrink, axis=0, keepdims=True)

    def stat_copy(shift):
        return pltpu.make_async_remote_copy(
            src_ref=stats.at[0],
            dst_ref=stats.at[cols - shift],
            send_sem=stat_send,
            recv_sem=stat_recv,
            device_id=at(in_row(shift)),
            device_id_type=MESH,
        )

    for shift in range(1, cols):
        stat_copy(shift).start()

    arrive(g_all, q_recv.at[1])
    arrive(stats, stat_recv)

    def turn(turned, slot):
        cut = (cols - slot) * tokens
        return jnp.concatenate([turned[:, cut:], turned[:, :cut]], axis=1)

    aligned = [stats[0]] + [turn(stats[slot], slot) for slot in range(1, cols)]
    top = functools.reduce(jnp.maximum, [part[0:1, :] for part in aligned])
    sums = functools.reduce(
        jnp.add, [jnp.exp2(part[0:1, :] - top) * part[1:2, :] for part in aligned]
    )
    inverse = 1.0 / sums

    def normalise(slot):
        if not (isinstance(slot, int) and slot == 0):
            arrived(1, slot)
        dprobs = dot(v_all[slot], g_all[...].reshape(queries, width), 1, 1)
        probs = p_all[slot] * (jnp.exp2(part_stat[slot, 0:1, :] - top) * inverse)
        low = probs.astype(jnp.bfloat16)
        p_all[slot] = probs
        p_low[slot] = low
        dp_all[slot] = dprobs
        part_stat[slot, 2:3, :] = jnp.sum(
            low.astype(jnp.float32) * dprobs, axis=0, keepdims=True
        )

    normalise(0)
    for_each(rows - 1, lambda i: normalise(i + 1))
    deltas[0] = jnp.sum(part_stat[:, 2, :], axis=0, keepdims=True)

    def delta_copy(shift):
        return pltpu.make_async_remote_copy(
            src_ref=deltas.at[0],
            dst_ref=deltas.at[cols - shift],
            send_sem=delta_send,
            recv_sem=delta_recv,
            device_id=at(in_row(shift)),
            device_id_type=MESH,
        )

    for shift in range(1, cols):
        delta_copy(shift).start()

    def column_out(which, slot):
        source, target = ((dk_out, dk_in), (dv_out, dv_in))[which]
        return pltpu.make_async_remote_copy(
            src_ref=source.at[slot],
            dst_ref=target.at[rows - slot],
            send_sem=kout_send.at[which],
            recv_sem=kout_recv.at[which],
            device_id=at(in_column(slot)),
            device_id_type=MESH,
        )

    def value_pass(slot):
        value_part = dot(p_low[slot], g_all[...].reshape(queries, width), 1, 0)
        if isinstance(slot, int) and slot == 0:
            dv_ref[...] = value_part
        else:
            dv_out[slot] = value_part.astype(jnp.bfloat16)
            column_out(1, slot).start()

    for_each(rows - 1, lambda i: value_pass(i + 1))

    def row_out(which, slot):
        source, target = ((o_out, o_in), (dq_out, dq_in))[which]
        return pltpu.make_async_remote_copy(
            src_ref=source.at[slot],
            dst_ref=target.at[cols - slot],
            send_sem=qout_send.at[which],
            recv_sem=qout_recv.at[which],
            device_id=at(in_row(slot)),
            device_id_type=MESH,
        )

    p_flat = p_low[...].reshape(rows * tokens, queries)
    v_flat = v_all[...].reshape(rows * tokens, width)
    out_part = dot(v_flat, p_flat, 0, 0)
    for slot in range(1, cols):
        o_out[slot] = out_part[:, slot * tokens : (slot + 1) * tokens].astype(jnp.bfloat16)
        row_out(0, slot).start()

    arrive(deltas, delta_recv)
    delta = deltas[0]
    for slot in range(1, cols):
        delta = delta + turn(deltas[slot], slot)

    def second_pass(slot):
        dscore = p_all[slot] * (dp_all[slot] - delta)
        ds = dscore.astype(jnp.bfloat16)
        ds_low[slot] = ds
        key_part = dot(ds, q_all[...].reshape(queries, width), 1, 0) * scale
        points = -to_row(jnp.sum(dscore, axis=1, keepdims=True))
        if isinstance(slot, int):
            pts_in[0, slot : slot + 1, :] = points
        else:
            pts_in[0, pl.ds(slot, 1), :] = points
        if isinstance(slot, int) and slot == 0:
            dk_ref[...] = key_part
        else:
            dk_out[slot] = key_part.astype(jnp.bfloat16)
            column_out(0, slot).start()

    for_each(rows - 1, lambda i: second_pass(i + 1))
    second_pass(0)
    value_pass(0)

    def pts_copy(shift):
        return pltpu.make_async_remote_copy(
            src_ref=pts_in.at[0],
            dst_ref=pts_in.at[shift],
            send_sem=pts_send,
            recv_sem=pts_recv,
            device_id=at(other(shift)),
            device_id_type=MESH,
        )

    lax.fori_loop(1, devices, lambda i, c: (pts_copy(i).start(), c)[1], 0)

    ds_flat = ds_low[...].reshape(rows * tokens, queries)
    k_flat = k_all[...].reshape(rows * tokens, width)
    query_part = dot(k_flat, ds_flat, 0, 0) * scale
    for slot in range(1, cols):
        dq_out[slot] = query_part[:, slot * tokens : (slot + 1) * tokens].astype(jnp.bfloat16)
        row_out(1, slot).start()

    arrive(o_in, qout_recv.at[0])
    out_sum = out_part[:, :tokens]
    for slot in range(1, cols):
        out_sum = out_sum + o_in[slot].astype(jnp.float32)
    out_ref[...] = jnp.transpose(out_sum).astype(out_ref.dtype)

    arrive(pts_in, pts_recv)

    def add_points(index, carry):
        later, own = carry
        row = index // cols
        col = index % cols
        point = jnp.zeros((1, tokens), jnp.float32)
        for s in range(rows):
            giver = lax.rem(row + rows - s, rows) * cols + col
            point = point + pts_in[slot_of(giver), s : s + 1, :]
        their_order = meta[slot_of(index), 1:2, :]
        for half in range(halves):
            later[half] = later[half] + jnp.where(
                their_order > order_ref[half].astype(jnp.float32), point, 0.0
            )
        return (later, jnp.where(index == me, point, own))

    carry = ([jnp.zeros((1, tokens), jnp.float32) for _ in range(halves)],) + (
        jnp.zeros((1, tokens), jnp.float32),
    )
    if devices <= 16:
        for index in range(devices):
            carry = add_points(index, carry)
    else:
        carry = lax.fori_loop(0, devices, add_points, carry)
    later, own = carry
    gate_grad = jnp.sum(jnp.where(same & (line >= lane), to_column(own), 0.0), axis=0, keepdims=True)
    for half in range(halves):
        rest = jnp.sum(later[half], axis=1, keepdims=True)
        gate_grad = jnp.where(lane_row // piece == half, gate_grad + rest, gate_grad)
    dgate_ref[...] = gate_grad.reshape(tokens)

    arrive(dq_in, qout_recv.at[1])
    query_sum = query_part[:, :tokens]
    for slot in range(1, cols):
        query_sum = query_sum + dq_in[slot].astype(jnp.float32)
    dq_ref[...] = jnp.transpose(query_sum)

    for which, target in enumerate((dk_ref, dv_ref)):
        arrive((dk_in, dv_in)[which], kout_recv.at[which])
        for slot in range(1, rows):
            target[...] += (dk_in, dv_in)[which][slot].astype(jnp.float32)

    arrive(meta, meta_send)
    arrive(pts_in, pts_send)
    arrive(stats, stat_send)
    arrive(deltas, delta_send)
    for which in range(2):
        arrive(q_all, q_send.at[which])
        arrive(k_all, k_send.at[which])
        arrive(o_in, qout_send.at[which])
        arrive(dk_in, kout_send.at[which])


def hand_on(count, *refs):
    sources, targets, sems = refs[:count], refs[count : 2 * count], refs[2 * count]
    copies = [
        pltpu.make_async_copy(source, target, sems.at[index])
        for index, (source, target) in enumerate(zip(sources, targets))
    ]
    for copy in copies:
        copy.start()
    for copy in copies:
        copy.wait()


def local(rows, cols, queries, keys, values, log_gate, out_grad, segment_order):
    tokens, width = queries.shape
    halves = segment_order.shape[0]
    devices = rows * cols
    across = cols * tokens
    low, full = jnp.bfloat16, jnp.float32
    dma = pltpu.SemaphoreType.DMA
    in_vmem = pl.BlockSpec(memory_space=pltpu.VMEM)
    in_hbm = pl.BlockSpec(memory_space=pltpu.HBM)
    shapes = (
        jax.ShapeDtypeStruct((tokens, width), low),
        jax.ShapeDtypeStruct((tokens, width), full),
        jax.ShapeDtypeStruct((tokens, width), full),
        jax.ShapeDtypeStruct((tokens, width), full),
        jax.ShapeDtypeStruct((tokens,), full),
    )
    results = pl.pallas_call(
        functools.partial(kernel, rows, cols, halves),
        out_shape=tuple(pltpu.VMEM(shape.shape, shape.dtype) for shape in shapes),
        in_specs=[in_hbm] * 5 + [pl.BlockSpec(memory_space=pltpu.SMEM)],
        out_specs=[in_vmem] * 5,
        scratch_shapes=[
            pltpu.VMEM((tokens,), full),
            dma((5,)),
            pltpu.VMEM((devices, 2, tokens), full),
            pltpu.VMEM((devices, rows, tokens), full),
            pltpu.VMEM((devices, tokens), full),
            pltpu.VMEM((devices, tokens), full),
            pltpu.VMEM((cols, tokens, width), low),
            pltpu.VMEM((cols, tokens, width), low),
            pltpu.VMEM((rows, tokens, width), low),
            pltpu.VMEM((rows, tokens, width), low),
            pltpu.VMEM((rows, tokens, across), full),
            pltpu.VMEM((rows, tokens, across), full),
            pltpu.VMEM((rows, 8, across), full),
            pltpu.VMEM((cols, 4, across), full),
            pltpu.VMEM((cols, 1, across), full),
            pltpu.VMEM((rows, tokens, across), low),
            pltpu.VMEM((rows, tokens, across), low),
            pltpu.VMEM((rows, tokens, width), low),
            pltpu.VMEM((rows, tokens, width), low),
            pltpu.VMEM((rows, tokens, width), low),
            pltpu.VMEM((rows, tokens, width), low),
            pltpu.VMEM((cols, tokens, width), low),
            pltpu.VMEM((cols, tokens, width), low),
            pltpu.VMEM((cols, tokens, width), low),
            pltpu.VMEM((cols, tokens, width), low),
            dma(()),
            dma(()),
            dma(()),
            dma(()),
            dma((2,)),
            dma((2,)),
            dma((2,)),
            dma((2, rows)),
            dma(()),
            dma(()),
            dma(()),
            dma(()),
            dma((2,)),
            dma((2,)),
            dma((2,)),
            dma((2,)),
        ],
        compiler_params=pltpu.CompilerParams(
            collective_id=0, has_side_effects=True, vmem_limit_bytes=60 * 1024 * 1024
        ),
    )(queries, keys, values, log_gate, out_grad, segment_order)
    return pl.pallas_call(
        functools.partial(hand_on, len(shapes)),
        out_shape=shapes,
        in_specs=[in_vmem] * len(shapes),
        out_specs=[in_hbm] * len(shapes),
        scratch_shapes=[dma((len(shapes),))],
        compiler_params=pltpu.CompilerParams(vmem_limit_bytes=1024 * 1024),
    )(*results)


def solution(mesh):
    devices = mesh.shape["seq"]
    cols = max(c for c in range(1, math.isqrt(devices) + 1) if devices % c == 0)
    flat = P(("grp", "seq"))
    wide = P(("grp", "seq"), None)
    return jax.shard_map(
        functools.partial(local, devices // cols, cols),
        mesh=mesh,
        in_specs=(wide, wide, wide, flat, wide, flat),
        out_specs=(wide, wide, wide, wide, flat),
        check_vma=False,
    )
```

```python
import functools
import math

import jax
import jax.numpy as jnp
from jax import lax
from jax.experimental import pallas as pl
from jax.experimental.pallas import tpu as pltpu
from jax.sharding import PartitionSpec as P

MESH = pl.DeviceIdType.MESH
HIDDEN = -1e30
FLOOR = -1e29
LOG2E = math.log2(math.e)


def dot(left, right, left_dim, right_dim):
    return lax.dot_general(
        left, right, (((left_dim,), (right_dim,)), ((), ())), preferred_element_type=jnp.float32
    )


def for_each(count, body):
    if count <= 4:
        for index in range(count):
            body(index)
    else:
        lax.fori_loop(0, count, lambda index, carry: (body(index), carry)[1], 0)


def kernel(
    rows,
    cols,
    halves,
    q_hbm,
    k_hbm,
    v_hbm,
    gate_hbm,
    g_hbm,
    order_ref,
    out_ref,
    dq_ref,
    dk_ref,
    dv_ref,
    dgate_ref,
    gate_ref,
    load_sems,
    meta,
    pts_in,
    cum,
    place,
    q_all,
    g_all,
    k_all,
    v_all,
    p_all,
    dp_all,
    part_stat,
    stats,
    deltas,
    p_low,
    ds_low,
    dk_out,
    dv_out,
    dk_in,
    dv_in,
    o_out,
    dq_out,
    o_in,
    dq_in,
    meta_send,
    meta_recv,
    pts_send,
    pts_recv,
    q_send,
    q_recv,
    k_send,
    k_recv,
    stat_send,
    stat_recv,
    delta_send,
    delta_recv,
    kout_send,
    kout_recv,
    qout_send,
    qout_recv,
):
    devices = rows * cols
    tokens, width = q_hbm.shape
    piece = tokens // halves
    queries = cols * tokens
    scale = width ** (-0.5)
    grp = lax.axis_index("grp")
    me = lax.axis_index("seq")
    my_row = me // cols
    my_col = me % cols

    def at(index):
        return (grp, index)

    def arrive(slots, sem, first=1):
        rest = slots.at[pl.ds(first, slots.shape[0] - first)]
        pltpu.make_async_copy(rest, rest, sem).wait()

    def in_row(shift):
        return my_row * cols + lax.rem(my_col + shift, cols)

    def in_column(shift):
        return lax.rem(my_row + shift, rows) * cols + my_col

    barrier = pltpu.get_barrier_semaphore()

    partners = [in_row(s) for s in range(1, cols)] + [in_column(s) for s in range(1, rows)]
    for partner in partners:
        pl.semaphore_signal(barrier, inc=1, device_id=at(partner), device_id_type=MESH)

    q_ref, g_ref, k_ref, v_ref = q_all.at[0], g_all.at[0], k_all.at[0], v_all.at[0]
    loads = [
        pltpu.make_async_copy(source, target, load_sems.at[index])
        for index, (source, target) in enumerate(
            (
                (gate_hbm, gate_ref),
                (q_hbm, q_ref),
                (k_hbm, k_ref),
                (g_hbm, g_ref),
                (v_hbm, v_ref),
            )
        )
    ]
    for load in loads:
        load.start()
    loads[0].wait()

    lane = lax.broadcasted_iota(jnp.int32, (tokens, tokens), 1)
    line = lax.broadcasted_iota(jnp.int32, (tokens, tokens), 0)
    same = lane // piece == line // piece
    diagonal = lane == line

    def to_column(row):
        return jnp.sum(jnp.where(diagonal, row, 0.0), axis=1, keepdims=True)

    def to_row(column):
        return jnp.sum(jnp.where(diagonal, column, 0.0), axis=0, keepdims=True)

    gate_row = gate_ref[...].reshape(1, tokens)
    local_cum = jnp.sum(
        jnp.where(same & (line <= lane), to_column(gate_row), 0.0), axis=0, keepdims=True
    )
    lane_row = lax.broadcasted_iota(jnp.int32, (1, tokens), 1)
    own_order = jnp.zeros((1, tokens), jnp.float32)
    for half in range(halves):
        own_order = jnp.where(
            lane_row // piece == half, order_ref[half].astype(jnp.float32), own_order
        )
    meta[0, 0:1, :] = local_cum
    meta[0, 1:2, :] = own_order
    for load in loads[1:]:
        load.wait()

    pl.semaphore_wait(barrier, len(partners))

    def meta_row_copy(shift):
        return pltpu.make_async_remote_copy(
            src_ref=meta.at[0],
            dst_ref=meta.at[cols - shift],
            send_sem=meta_send.at[0],
            recv_sem=meta_recv.at[0],
            device_id=at(in_row(shift)),
            device_id_type=MESH,
        )

    def meta_column_copy(shift):
        return pltpu.make_async_remote_copy(
            src_ref=meta.at[pl.ds(0, cols)],
            dst_ref=meta.at[pl.ds((rows - shift) * cols, cols)],
            send_sem=meta_send.at[1],
            recv_sem=meta_recv.at[1],
            device_id=at(in_column(shift)),
            device_id_type=MESH,
        )

    def row_copy(which, shift):
        ref, slots = ((q_ref, q_all), (g_ref, g_all))[which]
        return pltpu.make_async_remote_copy(
            src_ref=ref,
            dst_ref=slots.at[cols - shift],
            send_sem=q_send.at[which],
            recv_sem=q_recv.at[which],
            device_id=at(in_row(shift)),
            device_id_type=MESH,
        )

    def column_copy(which, shift):
        ref, slots = ((k_ref, k_all), (v_ref, v_all))[which]
        return pltpu.make_async_remote_copy(
            src_ref=ref,
            dst_ref=slots.at[rows - shift],
            send_sem=k_send.at[which],
            recv_sem=k_recv.at[which, rows - shift],
            device_id=at(in_column(shift)),
            device_id_type=MESH,
        )

    for shift in range(1, cols):
        meta_row_copy(shift).start()
    for shift in range(1, rows):
        column_copy(0, shift).start()
    for shift in range(1, cols):
        row_copy(0, shift).start()
    pltpu.make_async_copy(
        meta.at[pl.ds(1, cols - 1)], meta.at[pl.ds(1, cols - 1)], meta_recv.at[0]
    ).wait()
    for shift in range(1, rows):
        meta_column_copy(shift).start()
    for shift in range(1, rows):
        column_copy(1, shift).start()
    for shift in range(1, cols):
        row_copy(1, shift).start()

    arrive(meta, meta_recv.at[1], cols)

    orders = meta[:, 1, :]
    base = meta[:, 0, :]
    total = base
    for half in range(halves):
        totals = base[:, (half + 1) * piece - 1 : (half + 1) * piece]
        heads = orders[:, half * piece : half * piece + 1]

        for device in range(devices):
            earlier = heads[device : device + 1, :] < orders
            total = total + jnp.where(earlier, totals[device : device + 1, :], 0.0)
    cum[...] = total * LOG2E
    within = (lax.broadcasted_iota(jnp.int32, (devices, tokens), 1) % piece).astype(jnp.float32)
    place[...] = orders * piece + within

    query_cum = jnp.concatenate([cum[s : s + 1, :] for s in range(cols)], axis=1)
    query_place = jnp.concatenate([place[s : s + 1, :] for s in range(cols)], axis=1)

    arrive(q_all, q_recv.at[0])

    def first_pass(slot):
        source = slot * cols
        key_cum = to_column(cum[pl.ds(source, 1), :])
        key_place = to_column(place[pl.ds(source, 1), :])
        if isinstance(slot, int) and slot == 0:
            pass
        else:
            arrived(0, slot)
        scores = dot(k_all[slot], q_all[...].reshape(queries, width), 1, 1)
        scores = scores * (scale * LOG2E) + (query_cum - key_cum)
        scores = jnp.where(key_place <= query_place, scores, HIDDEN)
        top = jnp.maximum(jnp.max(scores, axis=0, keepdims=True), FLOOR)
        probs = jnp.exp2(scores - top)
        p_all[slot] = probs
        part_stat[slot, 0:1, :] = top
        part_stat[slot, 1:2, :] = jnp.sum(probs, axis=0, keepdims=True)

    def arrived(which, slot):
        ref, slots = ((k_ref, k_all), (v_ref, v_all))[which]
        pltpu.make_async_remote_copy(
            src_ref=ref,
            dst_ref=slots.at[slot],
            send_sem=k_send.at[which],
            recv_sem=k_recv.at[which, slot],
            device_id=at(in_column(slot)),
            device_id_type=MESH,
        ).wait_recv()

    first_pass(0)
    for_each(rows - 1, lambda i: first_pass(i + 1))

    tops = part_stat[:, 0, :]
    top = jnp.max(tops, axis=0, keepdims=True)
    shrink = jnp.exp2(tops - top)
    stats[0, 0:1, :] = top
    stats[0, 1:2, :] = jnp.sum(part_stat[:, 1, :] * shrink, axis=0, keepdims=True)

    def stat_copy(shift):
        return pltpu.make_async_remote_copy(
            src_ref=stats.at[0],
            dst_ref=stats.at[cols - shift],
            send_sem=stat_send,
            recv_sem=stat_recv,
            device_id=at(in_row(shift)),
            device_id_type=MESH,
        )

    for shift in range(1, cols):
        stat_copy(shift).start()

    arrive(g_all, q_recv.at[1])
    arrive(stats, stat_recv)

    def turn(turned, slot):
        cut = (cols - slot) * tokens
        return jnp.concatenate([turned[:, cut:], turned[:, :cut]], axis=1)

    aligned = [stats[0]] + [turn(stats[slot], slot) for slot in range(1, cols)]
    top = functools.reduce(jnp.maximum, [part[0:1, :] for part in aligned])
    sums = functools.reduce(
        jnp.add, [jnp.exp2(part[0:1, :] - top) * part[1:2, :] for part in aligned]
    )
    inverse = 1.0 / sums

    def normalise(slot):
        if not (isinstance(slot, int) and slot == 0):
            arrived(1, slot)
        dprobs = dot(v_all[slot], g_all[...].reshape(queries, width), 1, 1)
        probs = p_all[slot] * (jnp.exp2(part_stat[slot, 0:1, :] - top) * inverse)
        low = probs.astype(jnp.bfloat16)
        p_all[slot] = probs
        p_low[slot] = low
        dp_all[slot] = dprobs
        part_stat[slot, 2:3, :] = jnp.sum(
            low.astype(jnp.float32) * dprobs, axis=0, keepdims=True
        )

    normalise(0)
    for_each(rows - 1, lambda i: normalise(i + 1))
    deltas[0] = jnp.sum(part_stat[:, 2, :], axis=0, keepdims=True)

    def delta_copy(shift):
        return pltpu.make_async_remote_copy(
            src_ref=deltas.at[0],
            dst_ref=deltas.at[cols - shift],
            send_sem=delta_send,
            recv_sem=delta_recv,
            device_id=at(in_row(shift)),
            device_id_type=MESH,
        )

    for shift in range(1, cols):
        delta_copy(shift).start()

    def column_out(which, slot):
        source, target = ((dk_out, dk_in), (dv_out, dv_in))[which]
        return pltpu.make_async_remote_copy(
            src_ref=source.at[slot],
            dst_ref=target.at[rows - slot],
            send_sem=kout_send.at[which],
            recv_sem=kout_recv.at[which],
            device_id=at(in_column(slot)),
            device_id_type=MESH,
        )

    def value_pass(slot):
        value_part = dot(p_low[slot], g_all[...].reshape(queries, width), 1, 0)
        if isinstance(slot, int) and slot == 0:
            dv_ref[...] = value_part
        else:
            dv_out[slot] = value_part.astype(jnp.bfloat16)
            column_out(1, slot).start()

    for_each(rows - 1, lambda i: value_pass(i + 1))

    def row_out(which, slot):
        source, target = ((o_out, o_in), (dq_out, dq_in))[which]
        return pltpu.make_async_remote_copy(
            src_ref=source.at[slot],
            dst_ref=target.at[cols - slot],
            send_sem=qout_send.at[which],
            recv_sem=qout_recv.at[which],
            device_id=at(in_row(slot)),
            device_id_type=MESH,
        )

    p_flat = p_low[...].reshape(rows * tokens, queries)
    v_flat = v_all[...].reshape(rows * tokens, width)
    out_part = dot(v_flat, p_flat, 0, 0)
    for slot in range(1, cols):
        o_out[slot] = out_part[:, slot * tokens : (slot + 1) * tokens].astype(jnp.bfloat16)
        row_out(0, slot).start()

    arrive(deltas, delta_recv)
    delta = deltas[0]
    for slot in range(1, cols):
        delta = delta + turn(deltas[slot], slot)

    def second_pass(slot):
        dscore = p_all[slot] * (dp_all[slot] - delta)
        ds = dscore.astype(jnp.bfloat16)
        ds_low[slot] = ds
        key_part = dot(ds, q_all[...].reshape(queries, width), 1, 0) * scale
        points = -to_row(jnp.sum(dscore, axis=1, keepdims=True))
        if isinstance(slot, int):
            pts_in[0, slot : slot + 1, :] = points
        else:
            pts_in[0, pl.ds(slot, 1), :] = points
        if isinstance(slot, int) and slot == 0:
            dk_ref[...] = key_part
        else:
            dk_out[slot] = key_part.astype(jnp.bfloat16)
            column_out(0, slot).start()

    for_each(rows - 1, lambda i: second_pass(i + 1))
    second_pass(0)
    value_pass(0)

    def pts_row_copy(shift):
        return pltpu.make_async_remote_copy(
            src_ref=pts_in.at[0],
            dst_ref=pts_in.at[cols - shift],
            send_sem=pts_send.at[0],
            recv_sem=pts_recv.at[0],
            device_id=at(in_row(shift)),
            device_id_type=MESH,
        )

    def pts_column_copy(shift):
        return pltpu.make_async_remote_copy(
            src_ref=pts_in.at[pl.ds(0, cols)],
            dst_ref=pts_in.at[pl.ds((rows - shift) * cols, cols)],
            send_sem=pts_send.at[1],
            recv_sem=pts_recv.at[1],
            device_id=at(in_column(shift)),
            device_id_type=MESH,
        )

    for shift in range(1, cols):
        pts_row_copy(shift).start()

    ds_flat = ds_low[...].reshape(rows * tokens, queries)
    k_flat = k_all[...].reshape(rows * tokens, width)
    query_part = dot(k_flat, ds_flat, 0, 0) * scale
    for slot in range(1, cols):
        dq_out[slot] = query_part[:, slot * tokens : (slot + 1) * tokens].astype(jnp.bfloat16)
        row_out(1, slot).start()

    pltpu.make_async_copy(
        pts_in.at[pl.ds(1, cols - 1)], pts_in.at[pl.ds(1, cols - 1)], pts_recv.at[0]
    ).wait()
    for shift in range(1, rows):
        pts_column_copy(shift).start()

    arrive(o_in, qout_recv.at[0])
    out_sum = out_part[:, :tokens]
    for slot in range(1, cols):
        out_sum = out_sum + o_in[slot].astype(jnp.float32)
    out_ref[...] = jnp.transpose(out_sum).astype(out_ref.dtype)

    arrive(pts_in, pts_recv.at[1], cols)

    later = [jnp.zeros((1, tokens), jnp.float32) for _ in range(halves)]

    def points_of(row, col):
        return functools.reduce(
            jnp.add,
            [
                pts_in[r * cols + col, (row - r) % rows : (row - r) % rows + 1, :]
                for r in range(rows)
            ],
        )

    own = points_of(0, 0)
    for row in range(rows):
        for col in range(cols):
            point = own if row == col == 0 else points_of(row, col)
            their_order = meta[row * cols + col, 1:2, :]
            for half in range(halves):
                later[half] = later[half] + jnp.where(
                    their_order > order_ref[half].astype(jnp.float32), point, 0.0
                )
    gate_grad = jnp.sum(jnp.where(same & (line >= lane), to_column(own), 0.0), axis=0, keepdims=True)
    for half in range(halves):
        rest = jnp.sum(later[half], axis=1, keepdims=True)
        gate_grad = jnp.where(lane_row // piece == half, gate_grad + rest, gate_grad)
    dgate_ref[...] = gate_grad.reshape(tokens)

    arrive(dq_in, qout_recv.at[1])
    query_sum = query_part[:, :tokens]
    for slot in range(1, cols):
        query_sum = query_sum + dq_in[slot].astype(jnp.float32)
    dq_ref[...] = jnp.transpose(query_sum)

    for which, target in enumerate((dk_ref, dv_ref)):
        arrive((dk_in, dv_in)[which], kout_recv.at[which])
        for slot in range(1, rows):
            target[...] += (dk_in, dv_in)[which][slot].astype(jnp.float32)

    for buffer, sems in ((meta, meta_send), (pts_in, pts_send)):
        sent = buffer.at[pl.ds(1, cols - 1)]
        pltpu.make_async_copy(sent, sent, sems.at[0]).wait()
        arrive(buffer, sems.at[1], cols)
    arrive(stats, stat_send)
    arrive(deltas, delta_send)
    for which in range(2):
        arrive(q_all, q_send.at[which])
        arrive(k_all, k_send.at[which])
        arrive(o_in, qout_send.at[which])
        arrive(dk_in, kout_send.at[which])


def hand_on(count, *refs):
    sources, targets, sems = refs[:count], refs[count : 2 * count], refs[2 * count]
    copies = [
        pltpu.make_async_copy(source, target, sems.at[index])
        for index, (source, target) in enumerate(zip(sources, targets))
    ]
    for copy in copies:
        copy.start()
    for copy in copies:
        copy.wait()


def local(rows, cols, queries, keys, values, log_gate, out_grad, segment_order):
    tokens, width = queries.shape
    halves = segment_order.shape[0]
    devices = rows * cols
    across = cols * tokens
    low, full = jnp.bfloat16, jnp.float32
    dma = pltpu.SemaphoreType.DMA
    in_vmem = pl.BlockSpec(memory_space=pltpu.VMEM)
    in_hbm = pl.BlockSpec(memory_space=pltpu.HBM)
    shapes = (
        jax.ShapeDtypeStruct((tokens, width), low),
        jax.ShapeDtypeStruct((tokens, width), full),
        jax.ShapeDtypeStruct((tokens, width), full),
        jax.ShapeDtypeStruct((tokens, width), full),
        jax.ShapeDtypeStruct((tokens,), full),
    )
    results = pl.pallas_call(
        functools.partial(kernel, rows, cols, halves),
        out_shape=tuple(pltpu.VMEM(shape.shape, shape.dtype) for shape in shapes),
        in_specs=[in_hbm] * 5 + [pl.BlockSpec(memory_space=pltpu.SMEM)],
        out_specs=[in_vmem] * 5,
        scratch_shapes=[
            pltpu.VMEM((tokens,), full),
            dma((5,)),
            pltpu.VMEM((devices, 2, tokens), full),
            pltpu.VMEM((devices, rows, tokens), full),
            pltpu.VMEM((devices, tokens), full),
            pltpu.VMEM((devices, tokens), full),
            pltpu.VMEM((cols, tokens, width), low),
            pltpu.VMEM((cols, tokens, width), low),
            pltpu.VMEM((rows, tokens, width), low),
            pltpu.VMEM((rows, tokens, width), low),
            pltpu.VMEM((rows, tokens, across), full),
            pltpu.VMEM((rows, tokens, across), full),
            pltpu.VMEM((rows, 8, across), full),
            pltpu.VMEM((cols, 4, across), full),
            pltpu.VMEM((cols, 1, across), full),
            pltpu.VMEM((rows, tokens, across), low),
            pltpu.VMEM((rows, tokens, across), low),
            pltpu.VMEM((rows, tokens, width), low),
            pltpu.VMEM((rows, tokens, width), low),
            pltpu.VMEM((rows, tokens, width), low),
            pltpu.VMEM((rows, tokens, width), low),
            pltpu.VMEM((cols, tokens, width), low),
            pltpu.VMEM((cols, tokens, width), low),
            pltpu.VMEM((cols, tokens, width), low),
            pltpu.VMEM((cols, tokens, width), low),
            dma((2,)),
            dma((2,)),
            dma((2,)),
            dma((2,)),
            dma((2,)),
            dma((2,)),
            dma((2,)),
            dma((2, rows)),
            dma(()),
            dma(()),
            dma(()),
            dma(()),
            dma((2,)),
            dma((2,)),
            dma((2,)),
            dma((2,)),
        ],
        compiler_params=pltpu.CompilerParams(
            collective_id=0, has_side_effects=True, vmem_limit_bytes=60 * 1024 * 1024
        ),
    )(queries, keys, values, log_gate, out_grad, segment_order)
    return pl.pallas_call(
        functools.partial(hand_on, len(shapes)),
        out_shape=shapes,
        in_specs=[in_vmem] * len(shapes),
        out_specs=[in_hbm] * len(shapes),
        scratch_shapes=[dma((len(shapes),))],
        compiler_params=pltpu.CompilerParams(vmem_limit_bytes=1024 * 1024),
    )(*results)


def solution(mesh):
    devices = mesh.shape["seq"]
    cols = max(c for c in range(1, math.isqrt(devices) + 1) if devices % c == 0)
    flat = P(("grp", "seq"))
    wide = P(("grp", "seq"), None)
    return jax.shard_map(
        functools.partial(local, devices // cols, cols),
        mesh=mesh,
        in_specs=(wide, wide, wide, flat, wide, flat),
        out_specs=(wide, wide, wide, wide, flat),
        check_vma=False,
    )
```

```python
import functools
import math

import jax
import jax.numpy as jnp
from jax import lax
from jax.experimental import pallas as pl
from jax.experimental.pallas import tpu as pltpu
from jax.sharding import PartitionSpec as P

MESH = pl.DeviceIdType.MESH
HIDDEN = -1e30
FLOOR = -1e29
LOG2E = math.log2(math.e)


def dot(left, right, left_dim, right_dim):
    return lax.dot_general(
        left, right, (((left_dim,), (right_dim,)), ((), ())), preferred_element_type=jnp.float32
    )


def for_each(count, body):
    if count <= 4:
        for index in range(count):
            body(index)
    else:
        lax.fori_loop(0, count, lambda index, carry: (body(index), carry)[1], 0)


def kernel(
    rows,
    cols,
    halves,
    q_hbm,
    k_hbm,
    v_hbm,
    gate_hbm,
    g_hbm,
    order_ref,
    out_ref,
    dq_ref,
    dk_ref,
    dv_ref,
    dgate_ref,
    gate_ref,
    load_sems,
    meta,
    pts_in,
    cum,
    place,
    q_all,
    g_all,
    k_all,
    v_all,
    p_all,
    dp_all,
    part_stat,
    stats,
    deltas,
    p_low,
    ds_low,
    dk_out,
    dv_out,
    dk_in,
    dv_in,
    o_out,
    dq_out,
    o_in,
    dq_in,
    meta_send,
    meta_recv,
    pts_send,
    pts_recv,
    q_send,
    q_recv,
    k_send,
    k_recv,
    stat_send,
    stat_recv,
    delta_send,
    delta_recv,
    kout_send,
    kout_recv,
    qout_send,
    qout_recv,
):
    devices = rows * cols
    tokens, width = q_hbm.shape
    piece = tokens // halves
    queries = cols * tokens
    scale = width ** (-0.5)
    grp = lax.axis_index("grp")
    me = lax.axis_index("seq")
    my_row = me // cols
    my_col = me % cols

    def at(index):
        return (grp, index)

    def arrive(slots, sem, first=1):
        rest = slots.at[pl.ds(first, slots.shape[0] - first)]
        pltpu.make_async_copy(rest, rest, sem).wait()

    def in_row(shift):
        return my_row * cols + lax.rem(my_col + shift, cols)

    def in_column(shift):
        return lax.rem(my_row + shift, rows) * cols + my_col

    barrier = pltpu.get_barrier_semaphore()

    partners = [in_row(s) for s in range(1, cols)] + [in_column(s) for s in range(1, rows)]
    for partner in partners:
        pl.semaphore_signal(barrier, inc=1, device_id=at(partner), device_id_type=MESH)

    q_ref, g_ref, k_ref, v_ref = q_all.at[0], g_all.at[0], k_all.at[0], v_all.at[0]
    loads = [
        pltpu.make_async_copy(source, target, load_sems.at[index])
        for index, (source, target) in enumerate(
            (
                (gate_hbm, gate_ref),
                (q_hbm, q_ref),
                (k_hbm, k_ref),
                (g_hbm, g_ref),
                (v_hbm, v_ref),
            )
        )
    ]
    for load in loads:
        load.start()
    loads[0].wait()

    lane = lax.broadcasted_iota(jnp.int32, (tokens, tokens), 1)
    line = lax.broadcasted_iota(jnp.int32, (tokens, tokens), 0)
    same = lane // piece == line // piece
    diagonal = lane == line

    def to_column(row):
        return jnp.sum(jnp.where(diagonal, row, 0.0), axis=1, keepdims=True)

    def to_row(column):
        return jnp.sum(jnp.where(diagonal, column, 0.0), axis=0, keepdims=True)

    gate_row = gate_ref[...].reshape(1, tokens)
    local_cum = jnp.sum(
        jnp.where(same & (line <= lane), to_column(gate_row), 0.0), axis=0, keepdims=True
    )
    lane_row = lax.broadcasted_iota(jnp.int32, (1, tokens), 1)
    own_order = jnp.zeros((1, tokens), jnp.float32)
    for half in range(halves):
        own_order = jnp.where(
            lane_row // piece == half, order_ref[half].astype(jnp.float32), own_order
        )
    meta[0, 0:1, :] = local_cum
    meta[0, 1:2, :] = own_order
    for load in loads[1:]:
        load.wait()

    pl.semaphore_wait(barrier, len(partners))

    def meta_row_copy(shift):
        return pltpu.make_async_remote_copy(
            src_ref=meta.at[0],
            dst_ref=meta.at[cols - shift],
            send_sem=meta_send.at[0],
            recv_sem=meta_recv.at[0],
            device_id=at(in_row(shift)),
            device_id_type=MESH,
        )

    def meta_column_copy(shift):
        return pltpu.make_async_remote_copy(
            src_ref=meta.at[pl.ds(0, cols)],
            dst_ref=meta.at[pl.ds((rows - shift) * cols, cols)],
            send_sem=meta_send.at[1],
            recv_sem=meta_recv.at[1],
            device_id=at(in_column(shift)),
            device_id_type=MESH,
        )

    def row_copy(which, shift):
        ref, slots = ((q_ref, q_all), (g_ref, g_all))[which]
        return pltpu.make_async_remote_copy(
            src_ref=ref,
            dst_ref=slots.at[cols - shift],
            send_sem=q_send.at[which],
            recv_sem=q_recv.at[which],
            device_id=at(in_row(shift)),
            device_id_type=MESH,
        )

    def column_copy(which, shift):
        ref, slots = ((k_ref, k_all), (v_ref, v_all))[which]
        return pltpu.make_async_remote_copy(
            src_ref=ref,
            dst_ref=slots.at[rows - shift],
            send_sem=k_send.at[which],
            recv_sem=k_recv.at[which, rows - shift],
            device_id=at(in_column(shift)),
            device_id_type=MESH,
        )

    for shift in range(1, cols):
        meta_row_copy(shift).start()
    for shift in range(1, rows):
        column_copy(0, shift).start()
    for shift in range(1, cols):
        row_copy(0, shift).start()
    pltpu.make_async_copy(
        meta.at[pl.ds(1, cols - 1)], meta.at[pl.ds(1, cols - 1)], meta_recv.at[0]
    ).wait()
    for shift in range(1, rows):
        meta_column_copy(shift).start()
    for shift in range(1, rows):
        column_copy(1, shift).start()
    for shift in range(1, cols):
        row_copy(1, shift).start()

    arrive(meta, meta_recv.at[1], cols)

    orders = meta[:, 1, :]
    base = meta[:, 0, :]
    total = base
    for half in range(halves):
        totals = base[:, (half + 1) * piece - 1 : (half + 1) * piece]
        heads = orders[:, half * piece : half * piece + 1]

        for device in range(devices):
            earlier = heads[device : device + 1, :] < orders
            total = total + jnp.where(earlier, totals[device : device + 1, :], 0.0)
    cum[...] = total * LOG2E
    within = (lax.broadcasted_iota(jnp.int32, (devices, tokens), 1) % piece).astype(jnp.float32)
    place[...] = orders * piece + within

    query_cum = jnp.concatenate([cum[s : s + 1, :] for s in range(cols)], axis=1)
    query_place = jnp.concatenate([place[s : s + 1, :] for s in range(cols)], axis=1)

    arrive(q_all, q_recv.at[0])

    def first_pass(slot):
        source = slot * cols
        key_cum = to_column(cum[pl.ds(source, 1), :])
        key_place = to_column(place[pl.ds(source, 1), :])
        if isinstance(slot, int) and slot == 0:
            pass
        else:
            arrived(0, slot)
        scores = dot(k_all[slot], q_all[...].reshape(queries, width), 1, 1)
        scores = scores * (scale * LOG2E) + (query_cum - key_cum)
        scores = jnp.where(key_place <= query_place, scores, HIDDEN)
        top = jnp.maximum(jnp.max(scores, axis=0, keepdims=True), FLOOR)
        probs = jnp.exp2(scores - top)
        p_all[slot] = probs
        part_stat[slot, 0:1, :] = top
        part_stat[slot, 1:2, :] = jnp.sum(probs, axis=0, keepdims=True)

    def arrived(which, slot):
        ref, slots = ((k_ref, k_all), (v_ref, v_all))[which]
        pltpu.make_async_remote_copy(
            src_ref=ref,
            dst_ref=slots.at[slot],
            send_sem=k_send.at[which],
            recv_sem=k_recv.at[which, slot],
            device_id=at(in_column(slot)),
            device_id_type=MESH,
        ).wait_recv()

    first_pass(0)
    for_each(rows - 1, lambda i: first_pass(i + 1))

    tops = part_stat[:, 0, :]
    top = jnp.max(tops, axis=0, keepdims=True)
    shrink = jnp.exp2(tops - top)
    stats[0, 0:1, :] = top
    stats[0, 1:2, :] = jnp.sum(part_stat[:, 1, :] * shrink, axis=0, keepdims=True)

    def stat_copy(shift):
        return pltpu.make_async_remote_copy(
            src_ref=stats.at[0],
            dst_ref=stats.at[cols - shift],
            send_sem=stat_send,
            recv_sem=stat_recv,
            device_id=at(in_row(shift)),
            device_id_type=MESH,
        )

    for shift in range(1, cols):
        stat_copy(shift).start()

    arrive(g_all, q_recv.at[1])
    dp_all[0] = dot(v_all[0], g_all[...].reshape(queries, width), 1, 1)
    arrive(stats, stat_recv)

    def turn(turned, slot):
        cut = (cols - slot) * tokens
        return jnp.concatenate([turned[:, cut:], turned[:, :cut]], axis=1)

    aligned = [stats[0]] + [turn(stats[slot], slot) for slot in range(1, cols)]
    top = functools.reduce(jnp.maximum, [part[0:1, :] for part in aligned])
    sums = functools.reduce(
        jnp.add, [jnp.exp2(part[0:1, :] - top) * part[1:2, :] for part in aligned]
    )
    inverse = 1.0 / sums

    def column_out(which, slot):
        source, target = ((dk_out, dk_in), (dv_out, dv_in))[which]
        return pltpu.make_async_remote_copy(
            src_ref=source.at[slot],
            dst_ref=target.at[rows - slot],
            send_sem=kout_send.at[which],
            recv_sem=kout_recv.at[which],
            device_id=at(in_column(slot)),
            device_id_type=MESH,
        )

    def normalise(slot):
        probs = p_all[slot] * (jnp.exp2(part_stat[slot, 0:1, :] - top) * inverse)
        low = probs.astype(jnp.bfloat16)
        p_all[slot] = probs
        p_low[slot] = low

    def value_pass(slot):
        value_part = dot(p_low[slot], g_all[...].reshape(queries, width), 1, 0)
        if isinstance(slot, int) and slot == 0:
            dv_ref[...] = value_part
        else:
            dv_out[slot] = value_part.astype(jnp.bfloat16)
            column_out(1, slot).start()

    def remote_values(slot):
        normalise(slot)
        value_pass(slot)

    for_each(rows - 1, lambda i: remote_values(i + 1))
    normalise(0)

    def delta_pass(slot):
        if isinstance(slot, int) and slot == 0:
            dprobs = dp_all[0]
        else:
            arrived(1, slot)
            dprobs = dot(v_all[slot], g_all[...].reshape(queries, width), 1, 1)
            dp_all[slot] = dprobs
        part_stat[slot, 2:3, :] = jnp.sum(
            p_low[slot].astype(jnp.float32) * dprobs, axis=0, keepdims=True
        )

    delta_pass(0)
    for_each(rows - 1, lambda i: delta_pass(i + 1))
    deltas[0] = jnp.sum(part_stat[:, 2, :], axis=0, keepdims=True)

    def delta_copy(shift):
        return pltpu.make_async_remote_copy(
            src_ref=deltas.at[0],
            dst_ref=deltas.at[cols - shift],
            send_sem=delta_send,
            recv_sem=delta_recv,
            device_id=at(in_row(shift)),
            device_id_type=MESH,
        )

    for shift in range(1, cols):
        delta_copy(shift).start()

    def row_out(which, slot):
        source, target = ((o_out, o_in), (dq_out, dq_in))[which]
        return pltpu.make_async_remote_copy(
            src_ref=source.at[slot],
            dst_ref=target.at[cols - slot],
            send_sem=qout_send.at[which],
            recv_sem=qout_recv.at[which],
            device_id=at(in_row(slot)),
            device_id_type=MESH,
        )

    p_flat = p_low[...].reshape(rows * tokens, queries)
    v_flat = v_all[...].reshape(rows * tokens, width)
    out_part = dot(v_flat, p_flat, 0, 0)
    for slot in range(1, cols):
        o_out[slot] = out_part[:, slot * tokens : (slot + 1) * tokens].astype(jnp.bfloat16)
        row_out(0, slot).start()

    value_pass(0)
    arrive(deltas, delta_recv)
    delta = deltas[0]
    for slot in range(1, cols):
        delta = delta + turn(deltas[slot], slot)

    def second_pass(slot):
        dscore = p_all[slot] * (dp_all[slot] - delta)
        ds = dscore.astype(jnp.bfloat16)
        ds_low[slot] = ds
        key_part = dot(ds, q_all[...].reshape(queries, width), 1, 0) * scale
        points = -to_row(jnp.sum(dscore, axis=1, keepdims=True))
        if isinstance(slot, int):
            pts_in[0, slot : slot + 1, :] = points
        else:
            pts_in[0, pl.ds(slot, 1), :] = points
        if isinstance(slot, int) and slot == 0:
            dk_ref[...] = key_part
        else:
            dk_out[slot] = key_part.astype(jnp.bfloat16)
            column_out(0, slot).start()

    for_each(rows - 1, lambda i: second_pass(i + 1))
    second_pass(0)

    def pts_row_copy(shift):
        return pltpu.make_async_remote_copy(
            src_ref=pts_in.at[0],
            dst_ref=pts_in.at[cols - shift],
            send_sem=pts_send.at[0],
            recv_sem=pts_recv.at[0],
            device_id=at(in_row(shift)),
            device_id_type=MESH,
        )

    def pts_column_copy(shift):
        return pltpu.make_async_remote_copy(
            src_ref=pts_in.at[pl.ds(0, cols)],
            dst_ref=pts_in.at[pl.ds((rows - shift) * cols, cols)],
            send_sem=pts_send.at[1],
            recv_sem=pts_recv.at[1],
            device_id=at(in_column(shift)),
            device_id_type=MESH,
        )

    for shift in range(1, cols):
        pts_row_copy(shift).start()

    ds_flat = ds_low[...].reshape(rows * tokens, queries)
    k_flat = k_all[...].reshape(rows * tokens, width)
    query_part = dot(k_flat, ds_flat, 0, 0) * scale
    for slot in range(1, cols):
        dq_out[slot] = query_part[:, slot * tokens : (slot + 1) * tokens].astype(jnp.bfloat16)
        row_out(1, slot).start()

    pltpu.make_async_copy(
        pts_in.at[pl.ds(1, cols - 1)], pts_in.at[pl.ds(1, cols - 1)], pts_recv.at[0]
    ).wait()
    for shift in range(1, rows):
        pts_column_copy(shift).start()

    arrive(o_in, qout_recv.at[0])
    out_sum = out_part[:, :tokens]
    for slot in range(1, cols):
        out_sum = out_sum + o_in[slot].astype(jnp.float32)
    out_ref[...] = jnp.transpose(out_sum).astype(out_ref.dtype)

    arrive(pts_in, pts_recv.at[1], cols)

    later = [jnp.zeros((1, tokens), jnp.float32) for _ in range(halves)]

    def points_of(row, col):
        return functools.reduce(
            jnp.add,
            [
                pts_in[r * cols + col, (row - r) % rows : (row - r) % rows + 1, :]
                for r in range(rows)
            ],
        )

    own = points_of(0, 0)
    for row in range(rows):
        for col in range(cols):
            point = own if row == col == 0 else points_of(row, col)
            their_order = meta[row * cols + col, 1:2, :]
            for half in range(halves):
                later[half] = later[half] + jnp.where(
                    their_order > order_ref[half].astype(jnp.float32), point, 0.0
                )
    gate_grad = jnp.sum(jnp.where(same & (line >= lane), to_column(own), 0.0), axis=0, keepdims=True)
    for half in range(halves):
        rest = jnp.sum(later[half], axis=1, keepdims=True)
        gate_grad = jnp.where(lane_row // piece == half, gate_grad + rest, gate_grad)
    dgate_ref[...] = gate_grad.reshape(tokens)

    arrive(dq_in, qout_recv.at[1])
    query_sum = query_part[:, :tokens]
    for slot in range(1, cols):
        query_sum = query_sum + dq_in[slot].astype(jnp.float32)
    dq_ref[...] = jnp.transpose(query_sum)

    for which, target in ((1, dv_ref), (0, dk_ref)):
        arrive((dk_in, dv_in)[which], kout_recv.at[which])
        for slot in range(1, rows):
            target[...] += (dk_in, dv_in)[which][slot].astype(jnp.float32)

    for buffer, sems in ((meta, meta_send), (pts_in, pts_send)):
        sent = buffer.at[pl.ds(1, cols - 1)]
        pltpu.make_async_copy(sent, sent, sems.at[0]).wait()
        arrive(buffer, sems.at[1], cols)
    arrive(stats, stat_send)
    arrive(deltas, delta_send)
    for which in range(2):
        arrive(q_all, q_send.at[which])
        arrive(k_all, k_send.at[which])
        arrive(o_in, qout_send.at[which])
        arrive(dk_in, kout_send.at[which])


def hand_on(count, *refs):
    sources, targets, sems = refs[:count], refs[count : 2 * count], refs[2 * count]
    copies = [
        pltpu.make_async_copy(source, target, sems.at[index])
        for index, (source, target) in enumerate(zip(sources, targets))
    ]
    for copy in copies:
        copy.start()
    for copy in copies:
        copy.wait()


def local(rows, cols, queries, keys, values, log_gate, out_grad, segment_order):
    tokens, width = queries.shape
    halves = segment_order.shape[0]
    devices = rows * cols
    across = cols * tokens
    low, full = jnp.bfloat16, jnp.float32
    dma = pltpu.SemaphoreType.DMA
    in_vmem = pl.BlockSpec(memory_space=pltpu.VMEM)
    in_hbm = pl.BlockSpec(memory_space=pltpu.HBM)
    shapes = (
        jax.ShapeDtypeStruct((tokens, width), low),
        jax.ShapeDtypeStruct((tokens, width), full),
        jax.ShapeDtypeStruct((tokens, width), full),
        jax.ShapeDtypeStruct((tokens, width), full),
        jax.ShapeDtypeStruct((tokens,), full),
    )
    results = pl.pallas_call(
        functools.partial(kernel, rows, cols, halves),
        out_shape=tuple(pltpu.VMEM(shape.shape, shape.dtype) for shape in shapes),
        in_specs=[in_hbm] * 5 + [pl.BlockSpec(memory_space=pltpu.SMEM)],
        out_specs=[in_vmem] * 5,
        scratch_shapes=[
            pltpu.VMEM((tokens,), full),
            dma((5,)),
            pltpu.VMEM((devices, 2, tokens), full),
            pltpu.VMEM((devices, rows, tokens), full),
            pltpu.VMEM((devices, tokens), full),
            pltpu.VMEM((devices, tokens), full),
            pltpu.VMEM((cols, tokens, width), low),
            pltpu.VMEM((cols, tokens, width), low),
            pltpu.VMEM((rows, tokens, width), low),
            pltpu.VMEM((rows, tokens, width), low),
            pltpu.VMEM((rows, tokens, across), full),
            pltpu.VMEM((rows, tokens, across), full),
            pltpu.VMEM((rows, 8, across), full),
            pltpu.VMEM((cols, 4, across), full),
            pltpu.VMEM((cols, 1, across), full),
            pltpu.VMEM((rows, tokens, across), low),
            pltpu.VMEM((rows, tokens, across), low),
            pltpu.VMEM((rows, tokens, width), low),
            pltpu.VMEM((rows, tokens, width), low),
            pltpu.VMEM((rows, tokens, width), low),
            pltpu.VMEM((rows, tokens, width), low),
            pltpu.VMEM((cols, tokens, width), low),
            pltpu.VMEM((cols, tokens, width), low),
            pltpu.VMEM((cols, tokens, width), low),
            pltpu.VMEM((cols, tokens, width), low),
            dma((2,)),
            dma((2,)),
            dma((2,)),
            dma((2,)),
            dma((2,)),
            dma((2,)),
            dma((2,)),
            dma((2, rows)),
            dma(()),
            dma(()),
            dma(()),
            dma(()),
            dma((2,)),
            dma((2,)),
            dma((2,)),
            dma((2,)),
        ],
        compiler_params=pltpu.CompilerParams(
            collective_id=0, has_side_effects=True, vmem_limit_bytes=60 * 1024 * 1024
        ),
    )(queries, keys, values, log_gate, out_grad, segment_order)
    return pl.pallas_call(
        functools.partial(hand_on, len(shapes)),
        out_shape=shapes,
        in_specs=[in_vmem] * len(shapes),
        out_specs=[in_hbm] * len(shapes),
        scratch_shapes=[dma((len(shapes),))],
        compiler_params=pltpu.CompilerParams(vmem_limit_bytes=1024 * 1024),
    )(*results)


def solution(mesh):
    devices = mesh.shape["seq"]
    cols = max(c for c in range(1, math.isqrt(devices) + 1) if devices % c == 0)
    flat = P(("grp", "seq"))
    wide = P(("grp", "seq"), None)
    return jax.shard_map(
        functools.partial(local, devices // cols, cols),
        mesh=mesh,
        in_specs=(wide, wide, wide, flat, wide, flat),
        out_specs=(wide, wide, wide, wide, flat),
        check_vma=False,
    )
```

```python
import functools
import math

import jax
import jax.numpy as jnp
from jax import lax
from jax.experimental import pallas as pl
from jax.experimental.pallas import tpu as pltpu
from jax.sharding import PartitionSpec as P

MESH = pl.DeviceIdType.MESH
HIDDEN = -1e30
FLOOR = -1e29
LOG2E = math.log2(math.e)


def dot(left, right, left_dim, right_dim):
    return lax.dot_general(
        left, right, (((left_dim,), (right_dim,)), ((), ())), preferred_element_type=jnp.float32
    )


def for_each(count, body):
    if count <= 4:
        for index in range(count):
            body(index)
    else:
        lax.fori_loop(0, count, lambda index, carry: (body(index), carry)[1], 0)


def kernel(
    rows,
    cols,
    halves,
    q_hbm,
    k_hbm,
    v_hbm,
    gate_hbm,
    g_hbm,
    order_ref,
    out_ref,
    dq_ref,
    dk_ref,
    dv_ref,
    dgate_ref,
    gate_ref,
    load_sems,
    meta,
    pts_in,
    cum,
    place,
    q_all,
    g_all,
    k_all,
    v_all,
    p_all,
    dp_all,
    part_stat,
    stats,
    deltas,
    p_low,
    ds_low,
    dk_out,
    dv_out,
    dk_in,
    dv_in,
    o_out,
    dq_out,
    o_in,
    dq_in,
    meta_send,
    meta_recv,
    pts_send,
    pts_recv,
    q_send,
    q_recv,
    k_send,
    k_recv,
    stat_send,
    stat_recv,
    delta_send,
    delta_recv,
    kout_send,
    kout_recv,
    qout_send,
    qout_recv,
):
    devices = rows * cols
    tokens, width = q_hbm.shape
    piece = tokens // halves
    queries = cols * tokens
    scale = width ** (-0.5)
    grp = lax.axis_index("grp")
    me = lax.axis_index("seq")
    my_row = me // cols
    my_col = me % cols

    def at(index):
        return (grp, index)

    def arrive(slots, sem, first=1):
        rest = slots.at[pl.ds(first, slots.shape[0] - first)]
        pltpu.make_async_copy(rest, rest, sem).wait()

    def in_row(shift):
        return my_row * cols + lax.rem(my_col + shift, cols)

    def in_column(shift):
        return lax.rem(my_row + shift, rows) * cols + my_col

    barrier = pltpu.get_barrier_semaphore()

    partners = [in_row(s) for s in range(1, cols)] + [in_column(s) for s in range(1, rows)]
    for partner in partners:
        pl.semaphore_signal(barrier, inc=1, device_id=at(partner), device_id_type=MESH)

    q_ref, g_ref, k_ref, v_ref = q_all.at[0], g_all.at[0], k_all.at[0], v_all.at[0]
    loads = [
        pltpu.make_async_copy(source, target, load_sems.at[index])
        for index, (source, target) in enumerate(
            (
                (gate_hbm, gate_ref),
                (q_hbm, q_ref),
                (k_hbm, k_ref),
                (g_hbm, g_ref),
                (v_hbm, v_ref),
            )
        )
    ]
    for load in loads:
        load.start()
    loads[0].wait()

    lane = lax.broadcasted_iota(jnp.int32, (tokens, tokens), 1)
    line = lax.broadcasted_iota(jnp.int32, (tokens, tokens), 0)
    same = lane // piece == line // piece
    diagonal = lane == line

    def to_column(row):
        return jnp.sum(jnp.where(diagonal, row, 0.0), axis=1, keepdims=True)

    def to_row(column):
        return jnp.sum(jnp.where(diagonal, column, 0.0), axis=0, keepdims=True)

    gate_row = gate_ref[...].reshape(1, tokens)
    local_cum = jnp.sum(
        jnp.where(same & (line <= lane), to_column(gate_row), 0.0), axis=0, keepdims=True
    )
    lane_row = lax.broadcasted_iota(jnp.int32, (1, tokens), 1)
    own_order = jnp.zeros((1, tokens), jnp.float32)
    for half in range(halves):
        own_order = jnp.where(
            lane_row // piece == half, order_ref[half].astype(jnp.float32), own_order
        )
    meta[0, 0:1, :] = local_cum
    meta[0, 1:2, :] = own_order
    for load in loads[1:]:
        load.wait()

    pl.semaphore_wait(barrier, len(partners))

    def meta_row_copy(shift):
        return pltpu.make_async_remote_copy(
            src_ref=meta.at[0],
            dst_ref=meta.at[cols - shift],
            send_sem=meta_send.at[0],
            recv_sem=meta_recv.at[0],
            device_id=at(in_row(shift)),
            device_id_type=MESH,
        )

    def meta_column_copy(shift):
        return pltpu.make_async_remote_copy(
            src_ref=meta.at[pl.ds(0, cols)],
            dst_ref=meta.at[pl.ds((rows - shift) * cols, cols)],
            send_sem=meta_send.at[1],
            recv_sem=meta_recv.at[1],
            device_id=at(in_column(shift)),
            device_id_type=MESH,
        )

    def row_copy(which, shift):
        ref, slots = ((q_ref, q_all), (g_ref, g_all))[which]
        return pltpu.make_async_remote_copy(
            src_ref=ref,
            dst_ref=slots.at[cols - shift],
            send_sem=q_send.at[which],
            recv_sem=q_recv.at[which],
            device_id=at(in_row(shift)),
            device_id_type=MESH,
        )

    def column_copy(which, shift):
        ref, slots = ((k_ref, k_all), (v_ref, v_all))[which]
        return pltpu.make_async_remote_copy(
            src_ref=ref,
            dst_ref=slots.at[rows - shift],
            send_sem=k_send.at[which],
            recv_sem=k_recv.at[which, rows - shift],
            device_id=at(in_column(shift)),
            device_id_type=MESH,
        )

    for shift in range(1, cols):
        meta_row_copy(shift).start()
    for shift in range(1, rows):
        column_copy(0, shift).start()
    for shift in range(1, cols):
        row_copy(0, shift).start()
    pltpu.make_async_copy(
        meta.at[pl.ds(1, cols - 1)], meta.at[pl.ds(1, cols - 1)], meta_recv.at[0]
    ).wait()
    for shift in range(1, rows):
        meta_column_copy(shift).start()
    for shift in range(1, rows):
        column_copy(1, shift).start()
    for shift in range(1, cols):
        row_copy(1, shift).start()

    arrive(meta, meta_recv.at[1], cols)

    orders = meta[:, 1, :]
    base = meta[:, 0, :]
    total = base
    for half in range(halves):
        totals = base[:, (half + 1) * piece - 1 : (half + 1) * piece]
        totals = jnp.broadcast_to(totals, (devices, tokens))
        heads = jnp.broadcast_to(orders[:, half * piece : half * piece + 1], (devices, tokens))
        for device in range(devices):
            earlier = heads[device : device + 1, :] < orders
            total = total + jnp.where(earlier, totals[device : device + 1, :], 0.0)
    cum[...] = total * LOG2E
    within = (lax.broadcasted_iota(jnp.int32, (devices, tokens), 1) % piece).astype(jnp.float32)
    place[...] = orders * piece + within

    query_cum = jnp.concatenate([cum[s : s + 1, :] for s in range(cols)], axis=1)
    query_place = jnp.concatenate([place[s : s + 1, :] for s in range(cols)], axis=1)

    arrive(q_all, q_recv.at[0])

    def first_pass(slot):
        source = slot * cols
        key_cum = to_column(cum[pl.ds(source, 1), :])
        key_place = to_column(place[pl.ds(source, 1), :])
        if isinstance(slot, int) and slot == 0:
            pass
        else:
            arrived(0, slot)
        scores = dot(k_all[slot], q_all[...].reshape(queries, width), 1, 1)
        scores = scores * (scale * LOG2E) + (query_cum - key_cum)
        scores = jnp.where(key_place <= query_place, scores, HIDDEN)
        top = jnp.maximum(jnp.max(scores, axis=0, keepdims=True), FLOOR)
        probs = jnp.exp2(scores - top)
        p_all[slot] = probs
        part_stat[slot, 0:1, :] = top
        part_stat[slot, 1:2, :] = jnp.sum(probs, axis=0, keepdims=True)

    def arrived(which, slot):
        ref, slots = ((k_ref, k_all), (v_ref, v_all))[which]
        pltpu.make_async_remote_copy(
            src_ref=ref,
            dst_ref=slots.at[slot],
            send_sem=k_send.at[which],
            recv_sem=k_recv.at[which, slot],
            device_id=at(in_column(slot)),
            device_id_type=MESH,
        ).wait_recv()

    first_pass(0)
    for_each(rows - 1, lambda i: first_pass(i + 1))

    tops = part_stat[:, 0, :]
    top = jnp.max(tops, axis=0, keepdims=True)
    shrink = jnp.exp2(tops - top)
    stats[0, 0:1, :] = top
    stats[0, 1:2, :] = jnp.sum(part_stat[:, 1, :] * shrink, axis=0, keepdims=True)

    def stat_copy(shift):
        return pltpu.make_async_remote_copy(
            src_ref=stats.at[0],
            dst_ref=stats.at[cols - shift],
            send_sem=stat_send,
            recv_sem=stat_recv,
            device_id=at(in_row(shift)),
            device_id_type=MESH,
        )

    for shift in range(1, cols):
        stat_copy(shift).start()

    arrive(g_all, q_recv.at[1])
    dp_all[0] = dot(v_all[0], g_all[...].reshape(queries, width), 1, 1)
    arrive(stats, stat_recv)

    def turn(turned, slot):
        cut = (cols - slot) * tokens
        return jnp.concatenate([turned[:, cut:], turned[:, :cut]], axis=1)

    aligned = [stats[0]] + [turn(stats[slot], slot) for slot in range(1, cols)]
    top = functools.reduce(jnp.maximum, [part[0:1, :] for part in aligned])
    sums = functools.reduce(
        jnp.add, [jnp.exp2(part[0:1, :] - top) * part[1:2, :] for part in aligned]
    )
    inverse = 1.0 / sums

    def normalise(slot):
        if isinstance(slot, int) and slot == 0:
            dprobs = dp_all[0]
        else:
            arrived(1, slot)
            dprobs = dot(v_all[slot], g_all[...].reshape(queries, width), 1, 1)
            dp_all[slot] = dprobs
        probs = p_all[slot] * (jnp.exp2(part_stat[slot, 0:1, :] - top) * inverse)
        low = probs.astype(jnp.bfloat16)
        p_all[slot] = probs
        p_low[slot] = low
        part_stat[slot, 2:3, :] = jnp.sum(
            low.astype(jnp.float32) * dprobs, axis=0, keepdims=True
        )

    normalise(0)
    for_each(rows - 1, lambda i: normalise(i + 1))
    deltas[0] = jnp.sum(part_stat[:, 2, :], axis=0, keepdims=True)

    def delta_copy(shift):
        return pltpu.make_async_remote_copy(
            src_ref=deltas.at[0],
            dst_ref=deltas.at[cols - shift],
            send_sem=delta_send,
            recv_sem=delta_recv,
            device_id=at(in_row(shift)),
            device_id_type=MESH,
        )

    for shift in range(1, cols):
        delta_copy(shift).start()

    def column_out(which, slot):
        source, target = ((dk_out, dk_in), (dv_out, dv_in))[which]
        return pltpu.make_async_remote_copy(
            src_ref=source.at[slot],
            dst_ref=target.at[rows - slot],
            send_sem=kout_send.at[which],
            recv_sem=kout_recv.at[which],
            device_id=at(in_column(slot)),
            device_id_type=MESH,
        )

    def value_pass(slot):
        value_part = dot(p_low[slot], g_all[...].reshape(queries, width), 1, 0)
        if isinstance(slot, int) and slot == 0:
            dv_ref[...] = value_part
        else:
            dv_out[slot] = value_part.astype(jnp.bfloat16)
            column_out(1, slot).start()

    for_each(rows - 1, lambda i: value_pass(i + 1))

    def row_out(which, slot):
        source, target = ((o_out, o_in), (dq_out, dq_in))[which]
        return pltpu.make_async_remote_copy(
            src_ref=source.at[slot],
            dst_ref=target.at[cols - slot],
            send_sem=qout_send.at[which],
            recv_sem=qout_recv.at[which],
            device_id=at(in_row(slot)),
            device_id_type=MESH,
        )

    p_flat = p_low[...].reshape(rows * tokens, queries)
    v_flat = v_all[...].reshape(rows * tokens, width)
    out_part = dot(v_flat, p_flat, 0, 0)
    for slot in range(1, cols):
        o_out[slot] = out_part[:, slot * tokens : (slot + 1) * tokens].astype(jnp.bfloat16)
        row_out(0, slot).start()

    arrive(deltas, delta_recv)
    delta = deltas[0]
    for slot in range(1, cols):
        delta = delta + turn(deltas[slot], slot)

    def second_pass(slot):
        dscore = p_all[slot] * (dp_all[slot] - delta)
        ds = dscore.astype(jnp.bfloat16)
        ds_low[slot] = ds
        key_part = dot(ds, q_all[...].reshape(queries, width), 1, 0) * scale
        points = -to_row(jnp.sum(dscore, axis=1, keepdims=True))
        if isinstance(slot, int):
            pts_in[0, slot : slot + 1, :] = points
        else:
            pts_in[0, pl.ds(slot, 1), :] = points
        if isinstance(slot, int) and slot == 0:
            dk_ref[...] = key_part
        else:
            dk_out[slot] = key_part.astype(jnp.bfloat16)
            column_out(0, slot).start()

    for_each(rows - 1, lambda i: second_pass(i + 1))
    second_pass(0)
    value_pass(0)

    def pts_row_copy(shift):
        return pltpu.make_async_remote_copy(
            src_ref=pts_in.at[0],
            dst_ref=pts_in.at[cols - shift],
            send_sem=pts_send.at[0],
            recv_sem=pts_recv.at[0],
            device_id=at(in_row(shift)),
            device_id_type=MESH,
        )

    def pts_column_copy(shift):
        return pltpu.make_async_remote_copy(
            src_ref=pts_in.at[pl.ds(0, cols)],
            dst_ref=pts_in.at[pl.ds((rows - shift) * cols, cols)],
            send_sem=pts_send.at[1],
            recv_sem=pts_recv.at[1],
            device_id=at(in_column(shift)),
            device_id_type=MESH,
        )

    for shift in range(1, cols):
        pts_row_copy(shift).start()

    ds_flat = ds_low[...].reshape(rows * tokens, queries)
    k_flat = k_all[...].reshape(rows * tokens, width)
    query_part = dot(k_flat, ds_flat, 0, 0) * scale
    for slot in range(1, cols):
        dq_out[slot] = query_part[:, slot * tokens : (slot + 1) * tokens].astype(jnp.bfloat16)
        row_out(1, slot).start()

    pltpu.make_async_copy(
        pts_in.at[pl.ds(1, cols - 1)], pts_in.at[pl.ds(1, cols - 1)], pts_recv.at[0]
    ).wait()
    for shift in range(1, rows):
        pts_column_copy(shift).start()

    arrive(o_in, qout_recv.at[0])
    out_sum = out_part[:, :tokens]
    for slot in range(1, cols):
        out_sum = out_sum + o_in[slot].astype(jnp.float32)
    out_ref[...] = jnp.transpose(out_sum).astype(out_ref.dtype)

    arrive(pts_in, pts_recv.at[1], cols)

    later = [jnp.zeros((1, tokens), jnp.float32) for _ in range(halves)]

    def points_of(row, col):
        return functools.reduce(
            jnp.add,
            [
                pts_in[r * cols + col, (row - r) % rows : (row - r) % rows + 1, :]
                for r in range(rows)
            ],
        )

    own = points_of(0, 0)
    for row in range(rows):
        for col in range(cols):
            point = own if row == col == 0 else points_of(row, col)
            their_order = meta[row * cols + col, 1:2, :]
            for half in range(halves):
                later[half] = later[half] + jnp.where(
                    their_order > order_ref[half].astype(jnp.float32), point, 0.0
                )
    gate_grad = jnp.sum(jnp.where(same & (line >= lane), to_column(own), 0.0), axis=0, keepdims=True)
    for half in range(halves):
        rest = jnp.sum(later[half], axis=1, keepdims=True)
        gate_grad = jnp.where(lane_row // piece == half, gate_grad + rest, gate_grad)
    dgate_ref[...] = gate_grad.reshape(tokens)

    arrive(dq_in, qout_recv.at[1])
    query_sum = query_part[:, :tokens]
    for slot in range(1, cols):
        query_sum = query_sum + dq_in[slot].astype(jnp.float32)
    dq_ref[...] = jnp.transpose(query_sum)

    for which, target in ((1, dv_ref), (0, dk_ref)):
        arrive((dk_in, dv_in)[which], kout_recv.at[which])
        for slot in range(1, rows):
            target[...] += (dk_in, dv_in)[which][slot].astype(jnp.float32)

    for buffer, sems in ((meta, meta_send), (pts_in, pts_send)):
        sent = buffer.at[pl.ds(1, cols - 1)]
        pltpu.make_async_copy(sent, sent, sems.at[0]).wait()
        arrive(buffer, sems.at[1], cols)
    arrive(stats, stat_send)
    arrive(deltas, delta_send)
    for which in range(2):
        arrive(q_all, q_send.at[which])
        arrive(k_all, k_send.at[which])
        arrive(o_in, qout_send.at[which])
        arrive(dk_in, kout_send.at[which])


def hand_on(count, *refs):
    sources, targets, sems = refs[:count], refs[count : 2 * count], refs[2 * count]
    copies = [
        pltpu.make_async_copy(source, target, sems.at[index])
        for index, (source, target) in enumerate(zip(sources, targets))
    ]
    for copy in copies:
        copy.start()
    for copy in copies:
        copy.wait()


def local(rows, cols, queries, keys, values, log_gate, out_grad, segment_order):
    tokens, width = queries.shape
    halves = segment_order.shape[0]
    devices = rows * cols
    across = cols * tokens
    low, full = jnp.bfloat16, jnp.float32
    dma = pltpu.SemaphoreType.DMA
    in_vmem = pl.BlockSpec(memory_space=pltpu.VMEM)
    in_hbm = pl.BlockSpec(memory_space=pltpu.HBM)
    shapes = (
        jax.ShapeDtypeStruct((tokens, width), low),
        jax.ShapeDtypeStruct((tokens, width), full),
        jax.ShapeDtypeStruct((tokens, width), full),
        jax.ShapeDtypeStruct((tokens, width), full),
        jax.ShapeDtypeStruct((tokens,), full),
    )
    results = pl.pallas_call(
        functools.partial(kernel, rows, cols, halves),
        out_shape=tuple(pltpu.VMEM(shape.shape, shape.dtype) for shape in shapes),
        in_specs=[in_hbm] * 5 + [pl.BlockSpec(memory_space=pltpu.SMEM)],
        out_specs=[in_vmem] * 5,
        scratch_shapes=[
            pltpu.VMEM((tokens,), full),
            dma((5,)),
            pltpu.VMEM((devices, 2, tokens), full),
            pltpu.VMEM((devices, rows, tokens), full),
            pltpu.VMEM((devices, tokens), full),
            pltpu.VMEM((devices, tokens), full),
            pltpu.VMEM((cols, tokens, width), low),
            pltpu.VMEM((cols, tokens, width), low),
            pltpu.VMEM((rows, tokens, width), low),
            pltpu.VMEM((rows, tokens, width), low),
            pltpu.VMEM((rows, tokens, across), full),
            pltpu.VMEM((rows, tokens, across), full),
            pltpu.VMEM((rows, 8, across), full),
            pltpu.VMEM((cols, 4, across), full),
            pltpu.VMEM((cols, 1, across), full),
            pltpu.VMEM((rows, tokens, across), low),
            pltpu.VMEM((rows, tokens, across), low),
            pltpu.VMEM((rows, tokens, width), low),
            pltpu.VMEM((rows, tokens, width), low),
            pltpu.VMEM((rows, tokens, width), low),
            pltpu.VMEM((rows, tokens, width), low),
            pltpu.VMEM((cols, tokens, width), low),
            pltpu.VMEM((cols, tokens, width), low),
            pltpu.VMEM((cols, tokens, width), low),
            pltpu.VMEM((cols, tokens, width), low),
            dma((2,)),
            dma((2,)),
            dma((2,)),
            dma((2,)),
            dma((2,)),
            dma((2,)),
            dma((2,)),
            dma((2, rows)),
            dma(()),
            dma(()),
            dma(()),
            dma(()),
            dma((2,)),
            dma((2,)),
            dma((2,)),
            dma((2,)),
        ],
        compiler_params=pltpu.CompilerParams(
            collective_id=0, has_side_effects=True, vmem_limit_bytes=60 * 1024 * 1024
        ),
    )(queries, keys, values, log_gate, out_grad, segment_order)
    return pl.pallas_call(
        functools.partial(hand_on, len(shapes)),
        out_shape=shapes,
        in_specs=[in_vmem] * len(shapes),
        out_specs=[in_hbm] * len(shapes),
        scratch_shapes=[dma((len(shapes),))],
        compiler_params=pltpu.CompilerParams(vmem_limit_bytes=1024 * 1024),
    )(*results)


def solution(mesh):
    devices = mesh.shape["seq"]
    cols = max(c for c in range(1, math.isqrt(devices) + 1) if devices % c == 0)
    flat = P(("grp", "seq"))
    wide = P(("grp", "seq"), None)
    return jax.shard_map(
        functools.partial(local, devices // cols, cols),
        mesh=mesh,
        in_specs=(wide, wide, wide, flat, wide, flat),
        out_specs=(wide, wide, wide, wide, flat),
        check_vma=False,
    )
```
